1024 devices in a mesh: dp: 64 (over x, y), tensor: 16 (over z, core).
Axes of the slice: x: 8, y: 8, z: 8, core: 2. Of those that a mesh axis runs over, the one named last changes fastest.
Arguments:
- attn_output: bfloat16 [49152, 2560], P('dp', 'tensor'), may hold values from -6 to 6
- readout_vectors: bfloat16 [49152, 2560], P('dp', 'tensor'), may hold values from -0.0390625 to 0.0390625
- w_out: bfloat16 [2560, 2560], P('tensor'), may hold values from -0.125 to 0.125
- log_gap: bfloat16 [49152], P('dp'), may hold values from -0.8984375 to 0.8984375
- magnitude: bfloat16 [49152], P('dp'), may hold values from 0.29882812 to 3
- reward_sign: int32 [49152], P('dp'), may hold values from 0 to 1
- keep_mask: int32 [49152], P('dp'), may hold values 0 or 1
- move_plan: int32 [64, 64], replicated, may hold values from 0 to 12, as said below
Outputs:
- grad_shard: float32 [2560, 2560], P('tensor', 'dp')
- statistics: float32 [3], replicated
The draws below stay inside these ranges and needn't reach their ends.
Inputs may be any that keep to these rules, and one draw needn't show every extreme that they name: Data index i's live slots are its first sum_j move_plan[i, j] slots; they go in order, the first move_plan[i, 0] to index 0, the next move_plan[i, 1] to index 1, and so on. Every entry is at most 12; each column sums to at most 384, some column to exactly 384; some row sums to exactly 768.
All inputs are finite; a program needn't handle non-finite values. No bound on the sum of `keep_mask` on one device may be relied on, other than what follows from the above.
Results may differ from the reference program's by a relative error of at most 0.008.
Values may be sent and summed in bfloat16 or wider, within the bound.
No kernel may reach another device: no remote copies, remote signals or barrier semaphores. Data moves between devices by JAX's collectives and lax.ppermute only.
A program may use at most 64 MiB of HBM per device.

```python
import math
import jax
import jax.numpy as jnp
from jax import lax

OUT_W = 2560
LOCAL = 768
IN_W = 2560
TOKENS = 49152
N_DP = 64
N_TENSOR = 16


def draw_move_plan(key, part):
    key = jax.random.fold_in(key, 7)
    key_base, key_heavy, key_hot = jax.random.split(key, 3)
    slot_size = LOCAL // N_DP
    ceiling = LOCAL // 2
    base = jax.random.randint(key_base, (N_DP, N_DP), 0, slot_size + 1)
    heavy = jax.random.randint(key_heavy, (), 0, N_DP)
    hottest = jax.random.randint(key_hot, (), 0, N_DP)
    row_ids = jnp.arange(N_DP)
    base = jnp.where(row_ids[:, None] == heavy, slot_size, base)
    base = jnp.where(row_ids[None, :] == hottest, slot_size, base)
    rolled = jnp.roll(base, -heavy, axis=0)
    before = jnp.cumsum(rolled, axis=0) - rolled
    capped = jnp.minimum(rolled, jnp.maximum(ceiling - before, 0))
    return jnp.roll(capped, heavy, axis=0).astype(jnp.int32)


def set_ends(drawn, key, least, largest):
    dims = drawn.shape
    index_at = [jax.random.randint(jax.random.fold_in(key, axis), (), 0, dims[axis]) for axis in range(len(dims))]
    drawn = drawn.at[tuple(index_at)].set(least)
    longest = dims.index(max(dims))
    index_at[longest] = (index_at[longest] + 1) % dims[longest]
    return drawn.at[tuple(index_at)].set(largest)


def strengthened(values, key, source, target, blocks, factor):
    owner, partner = [(jnp.arange(values.shape[dim]) // (values.shape[dim] // blocks)).reshape([-1 if axis == dim else 1 for axis in range(values.ndim)]) for dim in (source, target)]
    chosen = jax.random.permutation(key, blocks)[partner]
    strong = (owner == chosen) | (owner == (partner + blocks // 2) % blocks)
    return jnp.where(strong, factor * values, values)


def block_scale(key, extent, cuts, smallest, high):
    gain = 1.0
    for dim, parts in cuts:
        steps = jax.random.uniform(jax.random.fold_in(jax.random.fold_in(key, 6), dim), (parts,), jnp.float32, smallest / len(cuts), high / len(cuts))
        gain = gain * jnp.repeat(jnp.exp(steps), extent[dim] // parts).reshape((-1,) + (1,) * (len(extent) - 1 - dim))
    return gain


def centred(rng, dims, scale, most, pieces=(), kind=jnp.bfloat16):
    drawn = scale * jax.random.normal(rng, dims, jnp.float32)
    if pieces:
        drawn = drawn * block_scale(rng, dims, pieces, -0.22, 0.18)
    return jnp.clip(drawn, -most, most).astype(kind)


def noise_with(rng, dims, scale, bound, shards, heavy, kind=jnp.bfloat16):
    drawn = scale * jax.random.normal(rng, dims, jnp.float32)
    if shards:
        drawn = drawn * block_scale(rng, dims, shards, -0.22, 0.18)
    return jnp.clip(strengthened(drawn, jax.random.fold_in(rng, 3), *heavy), -bound, bound).astype(kind)


def setup_inputs(seed: int = 0) -> dict:
    splits = jax.random.split(jax.random.key(seed), 9)
    return {
        "attn_output": centred(splits[0], (TOKENS, IN_W), 1.0, 6.0, ((0, 64), (1, 16))),
        "readout_vectors": noise_with(splits[1], (TOKENS, OUT_W), (64 * OUT_W) ** -0.5, 0.0390625, ((0, 64), (1, 16)), (0, 1, 64, 4.0)),
        "w_out": centred(splits[2], (IN_W, OUT_W), IN_W ** -0.5, 0.125, ((0, 16),)),
        "log_gap": centred(splits[3], (TOKENS,), 0.15, 0.8984375, ((0, 64),)),
        "magnitude": jnp.clip(jnp.exp(math.log(3.0) - 2.306499 * jax.random.uniform(splits[4], (TOKENS,), jnp.float32) ** block_scale(splits[4], (TOKENS,), ((0, 64),), -0.2, 0.2)), 0.29882812, 3.0).astype(jnp.bfloat16),
        "reward_sign": set_ends(jax.random.randint(splits[5], (TOKENS,), 0, 2), jax.random.fold_in(splits[5], 1), 0, 1).astype(jnp.int32),
        "keep_mask": set_ends((jax.random.randint(splits[6], (TOKENS,), 0, 4) < 3).astype(jnp.int32), jax.random.fold_in(splits[6], 1), 0, 1),
        "move_plan": draw_move_plan(jax.random.fold_in(splits[8], 71), 0),
    }


EPS_LOW = 0.2
EPS_HIGH = 0.28
LOSS_SCALE = 16384.0


def reference(attn_output, readout_vectors, w_out, log_gap, magnitude, reward_sign, keep_mask, move_plan):
    width = IN_W // N_TENSOR
    live_counts = jnp.sum(move_plan, axis=1).astype(jnp.int32)
    slot_ids = jnp.arange(TOKENS, dtype=jnp.int32) % LOCAL
    owner_live = jnp.repeat(live_counts, LOCAL)
    weight = ((slot_ids < owner_live).astype(jnp.int32) * keep_mask).astype(jnp.float32)
    divisor = jnp.maximum(jnp.sum(weight), 1.0)
    outputs = jnp.zeros((TOKENS, OUT_W), jnp.float32)
    for block_id in range(N_TENSOR):
        lower = block_id * width
        partial_y = jnp.dot(attn_output[:, lower:lower + width], w_out[lower:lower + width, :],
                            preferred_element_type=jnp.float32)
        outputs = outputs + partial_y.astype(jnp.bfloat16).astype(jnp.float32)
    log_shift = jnp.sum(outputs * readout_vectors.astype(jnp.float32), axis=1)
    advantage = (2 * reward_sign - 1).astype(jnp.float32) * magnitude.astype(jnp.float32)
    prob_ratio = jnp.exp(log_gap.astype(jnp.float32) + log_shift)
    base_ratio = jnp.exp(log_gap.astype(jnp.float32))
    clip_high = ((advantage > 0) & (base_ratio > 1.0 + EPS_HIGH)).astype(jnp.float32)
    clip_low = ((advantage < 0) & (base_ratio < 1.0 - EPS_LOW)).astype(jnp.float32)
    surrogate = jnp.minimum(prob_ratio * advantage,
                            jnp.clip(prob_ratio, 1.0 - EPS_LOW, 1.0 + EPS_HIGH) * advantage)
    statistics = jnp.stack([-jnp.sum(weight * surrogate) / divisor,
                            jnp.sum(weight * clip_high) / divisor,
                            jnp.sum(weight * clip_low) / divisor])
    coefficient = -LOSS_SCALE * weight * advantage * prob_ratio * (1.0 - clip_high - clip_low) / divisor
    upstream = (coefficient[:, None] * readout_vectors.astype(jnp.float32)).astype(jnp.bfloat16)
    grad_shard = lax.dot_general(attn_output, upstream, (((0,), (0,)), ((), ())),
                                 preferred_element_type=jnp.float32)
    return grad_shard, statistics
```

```python
import jax
import jax.numpy as jnp
from jax import lax
from jax.experimental import pallas as pl
from jax.experimental.pallas import tpu as pltpu
from jax.sharding import PartitionSpec as P

EPS_LOW = 0.2
EPS_HIGH = 0.28
LOSS_SCALE = 16384.0
N_DP = 64
N_TENSOR = 16
CHUNK_ROWS = 56
LANES = 128


def vmem_spec():
    return pl.BlockSpec(memory_space=pltpu.VMEM)


def grad_kernel(recv_ref, aux_ref, sums_ref, attn_ref, readout_ref, out_ref, scaled_ref, stats_ref):
    @pl.when(pl.program_id(0) == 0)
    def _():
        shift = jnp.sum(recv_ref[...], axis=0)
        gap, signed, base = aux_ref[0], aux_ref[1], aux_ref[2]
        ratio = jnp.exp(gap + shift)
        loss = jnp.sum(
            jnp.minimum(ratio * signed, jnp.clip(ratio, 1.0 - EPS_LOW, 1.0 + EPS_HIGH) * signed)
        )
        coefficient = base * ratio
        row = jnp.concatenate([coefficient[r : r + 1] for r in range(6)], axis=1)
        scaled_ref[...] = (attn_ref[...].astype(jnp.float32) * row).astype(jnp.bfloat16)
        lane = lax.broadcasted_iota(jnp.int32, (8, LANES), 1)
        is_loss = (lane == 35) | (lane == 39) | (lane == 43)
        value = jnp.where(is_loss, loss, jnp.broadcast_to(sums_ref[...], (8, LANES)))
        high = value.astype(jnp.bfloat16).astype(jnp.float32)
        middle = (value - high).astype(jnp.bfloat16).astype(jnp.float32)
        low = value - high - middle
        stats_ref[...] = jnp.where(lane < 36, high, jnp.where(lane < 40, middle, low))

    product = lax.dot_general(
        readout_ref[...],
        scaled_ref[...],
        (((1,), (1,)), ((), ())),
        preferred_element_type=jnp.float32,
    )
    for q in range(4):
        part = product[40 * q : 40 * q + 40]
        rest = part[:, LANES:]
        first = jnp.concatenate([rest[8 * k : 8 * k + 8] for k in range(4)], axis=1)
        second = jnp.concatenate([rest[32:40], stats_ref[:, 32:]], axis=1)
        out_ref[q] = jnp.concatenate([part[:, :LANES], first, second], axis=0).astype(jnp.bfloat16)


def finish_kernel(recv_ref, grad_ref, stats_ref):
    total = jnp.sum(recv_ref[...].astype(jnp.float32), axis=0)
    first, second = total[40:48], total[48:56]
    lane = lax.broadcasted_iota(jnp.int32, (1, LANES), 1)
    row = second[0:1]

    def pick(k):
        mine = (lane == 32 + k) | (lane == 36 + k) | (lane == 40 + k)
        return jnp.sum(jnp.where(mine, row, 0.0), axis=1, keepdims=True)

    divisor = jnp.maximum(pick(0), 1.0)
    rest = jnp.concatenate([first[:, 32 * k : 32 * k + 32] for k in range(4)] + [second[:, :32]], axis=0)
    grad_ref[...] = jnp.concatenate([total[:40], rest], axis=1) / divisor
    stats_ref[...] = (
        jnp.where(lane == 0, -pick(3), jnp.where(lane == 1, pick(1), jnp.where(lane == 2, pick(2), 0.0)))
        / divisor
    )


def body(
    attn_output, readout_vectors, w_out, log_gap, magnitude, reward_sign, keep_mask, move_plan
):
    local_rows, width = attn_output.shape
    attn_t, readout_t = attn_output.T, readout_vectors.T
    dp_index = lax.axis_index("dp")
    live_total = jnp.sum(lax.dynamic_slice_in_dim(move_plan, dp_index, 1, 0))
    slot_ids = jnp.arange(local_rows, dtype=jnp.int32)
    weight = ((slot_ids < live_total).astype(jnp.int32) * keep_mask).astype(jnp.float32)
    advantage = (2 * reward_sign - 1).astype(jnp.float32) * magnitude.astype(jnp.float32)
    gap = log_gap.astype(jnp.float32)
    base_ratio = jnp.exp(gap)
    clip_high = ((advantage > 0) & (base_ratio > 1.0 + EPS_HIGH)).astype(jnp.float32)
    clip_low = ((advantage < 0) & (base_ratio < 1.0 - EPS_LOW)).astype(jnp.float32)
    signed = weight * advantage
    base = -LOSS_SCALE * signed * (1.0 - clip_high - clip_low)
    aux = jnp.pad(jnp.stack([gap, signed, base]).reshape(3, 6, LANES), ((0, 0), (0, 2), (0, 0)))
    four = jnp.stack(
        [jnp.sum(weight), jnp.sum(weight * clip_high), jnp.sum(weight * clip_low), jnp.float32(0)]
    )
    sums = jnp.pad(jnp.tile(four, 3), (32, LANES - 44))[None]

    readout_all = lax.all_gather(readout_t, "tensor", axis=0, tiled=True)
    projected = lax.dot_general(
        w_out, readout_all, (((1,), (0,)), ((), ())), preferred_element_type=jnp.float32
    )
    partial_shift = jnp.sum(projected * attn_t.astype(jnp.float32), axis=0)
    mine = jnp.pad(partial_shift.reshape(6, LANES), ((0, 2), (0, 0)))
    shifts = lax.all_to_all(
        jnp.broadcast_to(mine[None], (N_TENSOR, 8, LANES)), "tensor", 0, 0, tiled=True
    )
    chunks = pl.pallas_call(
        grad_kernel,
        grid=(N_TENSOR,),
        in_specs=[
            pl.BlockSpec((N_TENSOR, 8, LANES), lambda k: (0, 0, 0)),
            pl.BlockSpec((3, 8, LANES), lambda k: (0, 0, 0)),
            pl.BlockSpec((1, LANES), lambda k: (0, 0)),
            pl.BlockSpec((width, local_rows), lambda k: (0, 0)),
            pl.BlockSpec((width, local_rows), lambda k: (k, 0)),
        ],
        out_specs=pl.BlockSpec((4, CHUNK_ROWS, LANES), lambda k: (k, 0, 0)),
        out_shape=jax.ShapeDtypeStruct((N_DP, CHUNK_ROWS, LANES), jnp.bfloat16),
        scratch_shapes=[
            pltpu.VMEM((width, local_rows), jnp.bfloat16),
            pltpu.VMEM((8, LANES), jnp.float32),
        ],
        compiler_params=pltpu.CompilerParams(vmem_limit_bytes=24 << 20),
    )(shifts, aux, sums, attn_t, readout_all)
    received = lax.all_to_all(chunks, "dp", 0, 0, tiled=True)
    grad_t, stats = pl.pallas_call(
        finish_kernel,
        in_specs=[vmem_spec()],
        out_specs=[vmem_spec(), vmem_spec()],
        out_shape=[
            jax.ShapeDtypeStruct((40, width), jnp.float32),
            jax.ShapeDtypeStruct((1, LANES), jnp.float32),
        ],
        compiler_params=pltpu.CompilerParams(vmem_limit_bytes=24 << 20),
    )(received)
    return grad_t.T, stats[0, :3]


def solution(mesh):
    placed = (
        P("dp", "tensor"),
        P("dp", "tensor"),
        P("tensor", None),
        P("dp"),
        P("dp"),
        P("dp"),
        P("dp"),
        P(),
    )
    return jax.shard_map(
        body, mesh=mesh, in_specs=placed, out_specs=(P("tensor", "dp"), P()), check_vma=False
    )
```

```python
import jax
import jax.numpy as jnp
from jax import lax
from jax.experimental import pallas as pl
from jax.experimental.pallas import tpu as pltpu
from jax.sharding import PartitionSpec as P

EPS_LOW = 0.2
EPS_HIGH = 0.28
LOSS_SCALE = 16384.0
N_DP = 64
N_TENSOR = 16
CHUNK_ROWS = 56
LANES = 128
N_Z = 8
NEAR = 7
STEPS = (0, -1, 1, -2, 2, -3, 3)


def vmem_spec():
    return pl.BlockSpec(memory_space=pltpu.VMEM)


def piece_index(place):
    device = lax.axis_index("tensor")
    core = device & 1
    if place < NEAR:
        step, side = STEPS[place], core
    elif place < 2 * NEAR:
        step, side = STEPS[place - NEAR], 1 - core
    else:
        step, side = 4, (core, 1 - core)[place - 2 * NEAR]
    return (((device >> 1) + N_Z + step) & (N_Z - 1)) * 2 + side


def prepare_kernel(w_ref, gap_ref, size_ref, sign_ref, keep_ref, plan_ref, out_ref, aux_ref, sums_ref):
    width = out_ref.shape[2]
    for k in range(N_TENSOR):
        out_ref[k] = w_ref[:, width * k : width * k + width]
    owner = lax.broadcasted_iota(jnp.int32, plan_ref.shape, 0)
    live_total = jnp.sum(jnp.where(owner == lax.axis_index("dp"), plan_ref[...], 0))
    shape = gap_ref.shape
    slot_ids = lax.broadcasted_iota(jnp.int32, shape, 0) * LANES + lax.broadcasted_iota(jnp.int32, shape, 1)
    weight = jnp.where(slot_ids < live_total, keep_ref[...], 0).astype(jnp.float32)
    gap = gap_ref[...]
    advantage = (2 * sign_ref[...] - 1).astype(jnp.float32) * size_ref[...]
    base_ratio = jnp.exp(gap)
    clip_high = jnp.where((advantage > 0) & (base_ratio > 1.0 + EPS_HIGH), 1.0, 0.0)
    clip_low = jnp.where((advantage < 0) & (base_ratio < 1.0 - EPS_LOW), 1.0, 0.0)
    signed = weight * advantage
    zeros = jnp.zeros((2, LANES), jnp.float32)
    base = -LOSS_SCALE * signed * (1.0 - clip_high - clip_low)
    for k, value in enumerate((gap, signed, base)):
        aux_ref[k] = jnp.concatenate([value, zeros], axis=0)
    lane = lax.broadcasted_iota(jnp.int32, (8, LANES), 1)
    which = jnp.where((lane >= 32) & (lane < 44), lane & 3, 3)
    count, high, low = jnp.sum(weight), jnp.sum(weight * clip_high), jnp.sum(weight * clip_low)
    sums_ref[...] = jnp.where(
        which == 0, count, jnp.where(which == 1, high, jnp.where(which == 2, low, 0.0))
    )


def project(w_ref, places, pieces):
    total = None
    for place, piece in zip(places, pieces):
        product = jnp.dot(w_ref[piece_index(place)], piece, preferred_element_type=jnp.float32)
        total = product if total is None else total + product
    return total


def first_kernel(w_ref, mine_ref, out_ref):
    width = w_ref.shape[1]
    pieces = [mine_ref[width * k : width * k + width] for k in range(NEAR)]
    out_ref[...] = project(w_ref, range(NEAR), pieces)


def shift_kernel(w_ref, attn_ref, first_ref, other_ref, far_ref, far_other_ref, out_ref):
    width = w_ref.shape[1]
    pieces = [other_ref[width * k : width * k + width] for k in range(NEAR)]
    pieces += [far_ref[...], far_other_ref[...]]
    total = first_ref[...] + project(w_ref, range(NEAR, N_TENSOR), pieces)
    row = jnp.sum(total * attn_ref[...].astype(jnp.float32), axis=0, keepdims=True)
    rows = [row[:, LANES * r : LANES * r + LANES] for r in range(6)]
    block = jnp.concatenate(rows + [jnp.zeros((2, LANES), jnp.float32)], axis=0)
    for k in range(N_TENSOR):
        out_ref[k] = block


def grad_kernel(
    recv_ref,
    aux_ref,
    sums_ref,
    attn_ref,
    mine_ref,
    other_ref,
    far_ref,
    far_other_ref,
    out_ref,
):
    width = attn_ref.shape[0]
    shift = jnp.sum(recv_ref[...], axis=0)
    gap, signed, base = aux_ref[0], aux_ref[1], aux_ref[2]
    ratio = jnp.exp(gap + shift)
    loss = jnp.sum(
        jnp.minimum(ratio * signed, jnp.clip(ratio, 1.0 - EPS_LOW, 1.0 + EPS_HIGH) * signed)
    )
    coefficient = base * ratio
    row = jnp.concatenate([coefficient[r : r + 1] for r in range(6)], axis=1)
    scaled = (attn_ref[...].astype(jnp.float32) * row).astype(jnp.bfloat16)
    lane = lax.broadcasted_iota(jnp.int32, (8, LANES), 1)
    is_loss = (lane == 35) | (lane == 39) | (lane == 43)
    value = jnp.where(is_loss, loss, sums_ref[...])
    high = value.astype(jnp.bfloat16).astype(jnp.float32)
    middle = (value - high).astype(jnp.bfloat16).astype(jnp.float32)
    low = value - high - middle
    stats = jnp.where(lane < 36, high, jnp.where(lane < 40, middle, low))[:, 32:]
    for place in range(N_TENSOR):
        if place < NEAR:
            piece = mine_ref[width * place : width * place + width]
        elif place < 2 * NEAR:
            k = place - NEAR
            piece = other_ref[width * k : width * k + width]
        else:
            piece = (far_ref, far_other_ref)[place - 2 * NEAR][...]
        product = lax.dot_general(
            piece, scaled, (((1,), (1,)), ((), ())), preferred_element_type=jnp.float32
        )
        block = piece_index(place)
        for q in range(4):
            part = product[40 * q : 40 * q + 40]
            rest = part[:, LANES:]
            first = jnp.concatenate([rest[8 * k : 8 * k + 8] for k in range(4)], axis=1)
            second = jnp.concatenate([rest[32:40], stats], axis=1)
            out_ref[4 * block + q] = jnp.concatenate([part[:, :LANES], first, second], axis=0).astype(
                jnp.bfloat16
            )


def finish_kernel(recv_ref, grad_ref, stats_ref):
    total = jnp.sum(recv_ref[...].astype(jnp.float32), axis=0)
    first, second = total[40:48], total[48:56]
    lane = lax.broadcasted_iota(jnp.int32, (1, LANES), 1)
    row = second[0:1]

    def pick(k):
        mine = (lane == 32 + k) | (lane == 36 + k) | (lane == 40 + k)
        return jnp.sum(jnp.where(mine, row, 0.0), axis=1, keepdims=True)

    divisor = jnp.maximum(pick(0), 1.0)
    rest = jnp.concatenate([first[:, 32 * k : 32 * k + 32] for k in range(4)] + [second[:, :32]], axis=0)
    grad_ref[...] = jnp.concatenate([total[:40], rest], axis=1) / divisor
    stats_ref[...] = (
        jnp.where(lane == 0, -pick(3), jnp.where(lane == 1, pick(1), jnp.where(lane == 2, pick(2), 0.0)))
        / divisor
    )


def body(
    attn_output, readout_vectors, w_out, log_gap, magnitude, reward_sign, keep_mask, move_plan
):
    local_rows, width = attn_output.shape
    attn_t, readout_t = attn_output.T, readout_vectors.T
    up, down, cross, swap = [], [], [], []
    for z in range(N_Z):
        for c in range(2):
            up.append((2 * z + c, 2 * ((z + 1) % N_Z) + c))
            down.append((2 * ((z + 1) % N_Z) + c, 2 * z + c))
            cross.append((2 * ((z + 1) % N_Z) + 1 - c, 2 * z + c))
            swap.append((2 * z + 1 - c, 2 * z + c))
    rising, falling, nearby = readout_t, readout_t, [readout_t]
    for _ in range(3):
        rising = lax.ppermute(rising, "tensor", up)
        falling = lax.ppermute(falling, "tensor", down)
        nearby += [rising, falling]
    far_mine = lax.ppermute(rising, "tensor", up)
    far_other = lax.ppermute(falling, "tensor", cross)
    mine = jnp.concatenate(nearby, axis=0)
    other = lax.ppermute(mine, "tensor", swap)

    params = pltpu.CompilerParams(vmem_limit_bytes=24 << 20)
    tiled = (local_rows // LANES, LANES)
    w_blocks, aux, sums = pl.pallas_call(
        prepare_kernel,
        in_specs=[vmem_spec()] * 6,
        out_specs=[vmem_spec()] * 3,
        out_shape=[
            jax.ShapeDtypeStruct((N_TENSOR, width, width), w_out.dtype),
            jax.ShapeDtypeStruct((3, 8, LANES), jnp.float32),
            jax.ShapeDtypeStruct((8, LANES), jnp.float32),
        ],
        compiler_params=params,
    )(
        w_out,
        log_gap.astype(jnp.float32).reshape(tiled),
        magnitude.astype(jnp.float32).reshape(tiled),
        reward_sign.reshape(tiled),
        keep_mask.reshape(tiled),
        move_plan,
    )
    first = pl.pallas_call(
        first_kernel,
        in_specs=[vmem_spec()] * 2,
        out_specs=vmem_spec(),
        out_shape=jax.ShapeDtypeStruct((width, local_rows), jnp.float32),
        compiler_params=params,
    )(w_blocks, mine)
    partial_shift = pl.pallas_call(
        shift_kernel,
        in_specs=[vmem_spec()] * 6,
        out_specs=vmem_spec(),
        out_shape=jax.ShapeDtypeStruct((N_TENSOR, 8, LANES), jnp.float32),
        compiler_params=params,
    )(w_blocks, attn_t, first, other, far_mine, far_other)
    shifts = lax.all_to_all(partial_shift, "tensor", 0, 0, tiled=True)
    chunks = pl.pallas_call(
        grad_kernel,
        in_specs=[vmem_spec()] * 8,
        out_specs=vmem_spec(),
        out_shape=jax.ShapeDtypeStruct((N_DP, CHUNK_ROWS, LANES), jnp.bfloat16),
        compiler_params=params,
    )(shifts, aux, sums, attn_t, mine, other, far_mine, far_other)
    received = lax.all_to_all(chunks, "dp", 0, 0, tiled=True)
    grad_t, stats = pl.pallas_call(
        finish_kernel,
        in_specs=[vmem_spec()],
        out_specs=[vmem_spec(), vmem_spec()],
        out_shape=[
            jax.ShapeDtypeStruct((40, width), jnp.float32),
            jax.ShapeDtypeStruct((1, LANES), jnp.float32),
        ],
        compiler_params=pltpu.CompilerParams(vmem_limit_bytes=24 << 20),
    )(received)
    return grad_t.T, stats[0, :3]


def solution(mesh):
    placed = (
        P("dp", "tensor"),
        P("dp", "tensor"),
        P("tensor", None),
        P("dp"),
        P("dp"),
        P("dp"),
        P("dp"),
        P(),
    )
    return jax.shard_map(
        body, mesh=mesh, in_specs=placed, out_specs=(P("tensor", "dp"), P()), check_vma=False
    )
```

```python
import jax
import jax.numpy as jnp
from jax import lax
from jax.experimental import pallas as pl
from jax.experimental.pallas import tpu as pltpu
from jax.sharding import PartitionSpec as P

EPS_LOW = 0.2
EPS_HIGH = 0.28
LOSS_SCALE = 16384.0
N_DP = 64
N_TENSOR = 16
CHUNK_ROWS = 56
LANES = 128
N_Z = 8
NEAR = 7
STEPS = (0, -1, 1, -2, 2, -3, 3)


def vmem_spec():
    return pl.BlockSpec(memory_space=pltpu.VMEM)


def piece_index(place):
    device = lax.axis_index("tensor")
    core = device & 1
    if place < NEAR:
        step, side = STEPS[place], core
    elif place < 2 * NEAR:
        step, side = STEPS[place - NEAR], 1 - core
    else:
        step, side = 4, (core, 1 - core)[place - 2 * NEAR]
    return (((device >> 1) + N_Z + step) & (N_Z - 1)) * 2 + side


def prepare_kernel(w_ref, gap_ref, size_ref, sign_ref, keep_ref, plan_ref, out_ref, aux_ref, sums_ref):
    width = out_ref.shape[2]
    for k in range(N_TENSOR):
        out_ref[k] = w_ref[:, width * k : width * k + width]
    owner = lax.broadcasted_iota(jnp.int32, plan_ref.shape, 0)
    live_total = jnp.sum(jnp.where(owner == lax.axis_index("dp"), plan_ref[...], 0))
    shape = gap_ref.shape
    slot_ids = lax.broadcasted_iota(jnp.int32, shape, 0) * LANES + lax.broadcasted_iota(jnp.int32, shape, 1)
    weight = jnp.where(slot_ids < live_total, keep_ref[...], 0).astype(jnp.float32)
    gap = gap_ref[...]
    advantage = (2 * sign_ref[...] - 1).astype(jnp.float32) * size_ref[...]
    base_ratio = jnp.exp(gap)
    clip_high = jnp.where((advantage > 0) & (base_ratio > 1.0 + EPS_HIGH), 1.0, 0.0)
    clip_low = jnp.where((advantage < 0) & (base_ratio < 1.0 - EPS_LOW), 1.0, 0.0)
    signed = weight * advantage
    zeros = jnp.zeros((2, LANES), jnp.float32)
    base = -LOSS_SCALE * signed * (1.0 - clip_high - clip_low)
    for k, value in enumerate((gap, signed, base)):
        aux_ref[k] = jnp.concatenate([value, zeros], axis=0)
    lane = lax.broadcasted_iota(jnp.int32, (8, LANES), 1)
    which = jnp.where((lane >= 32) & (lane < 44), lane & 3, 3)
    count, high, low = jnp.sum(weight), jnp.sum(weight * clip_high), jnp.sum(weight * clip_low)
    sums_ref[...] = jnp.where(
        which == 0, count, jnp.where(which == 1, high, jnp.where(which == 2, low, 0.0))
    )


def project(w_ref, places, pieces):
    total = None
    for place, piece in zip(places, pieces):
        product = jnp.dot(w_ref[piece_index(place)], piece, preferred_element_type=jnp.float32)
        total = product if total is None else total + product
    return total


def first_kernel(w_ref, *refs):
    piece_refs, (out_ref, mine_ref) = refs[:NEAR], refs[NEAR:]
    width = w_ref.shape[1]
    pieces = [piece_ref[...] for piece_ref in piece_refs]
    out_ref[...] = project(w_ref, range(NEAR), pieces)
    for side in range(2):
        for k, piece in enumerate(pieces):
            mine_ref[side, width * k : width * k + width] = piece


def shift_kernel(w_ref, attn_ref, first_ref, pair_ref, far_ref, far_other_ref, out_ref):
    width = w_ref.shape[1]
    side = 1 - (lax.axis_index("tensor") & 1)
    pieces = [pair_ref[side, width * k : width * k + width] for k in range(NEAR)]
    pieces += [far_ref[...], far_other_ref[...]]
    total = first_ref[...] + project(w_ref, range(NEAR, N_TENSOR), pieces)
    row = jnp.sum(total * attn_ref[...].astype(jnp.float32), axis=0, keepdims=True)
    rows = [row[:, LANES * r : LANES * r + LANES] for r in range(6)]
    block = jnp.concatenate(rows + [jnp.zeros((2, LANES), jnp.float32)], axis=0)
    for k in range(N_TENSOR):
        out_ref[k] = block


def grad_kernel(
    recv_ref,
    aux_ref,
    sums_ref,
    attn_ref,
    pair_ref,
    far_ref,
    far_other_ref,
    out_ref,
):
    width = attn_ref.shape[0]
    core = lax.axis_index("tensor") & 1
    shift = jnp.sum(recv_ref[...], axis=0)
    gap, signed, base = aux_ref[0], aux_ref[1], aux_ref[2]
    ratio = jnp.exp(gap + shift)
    loss = jnp.sum(
        jnp.minimum(ratio * signed, jnp.clip(ratio, 1.0 - EPS_LOW, 1.0 + EPS_HIGH) * signed)
    )
    coefficient = base * ratio
    row = jnp.concatenate([coefficient[r : r + 1] for r in range(6)], axis=1)
    scaled = (attn_ref[...].astype(jnp.float32) * row).astype(jnp.bfloat16)
    lane = lax.broadcasted_iota(jnp.int32, (8, LANES), 1)
    is_loss = (lane == 35) | (lane == 39) | (lane == 43)
    value = jnp.where(is_loss, loss, sums_ref[...])
    high = value.astype(jnp.bfloat16).astype(jnp.float32)
    middle = (value - high).astype(jnp.bfloat16).astype(jnp.float32)
    low = value - high - middle
    stats = jnp.where(lane < 36, high, jnp.where(lane < 40, middle, low))[:, 32:]
    for place in range(N_TENSOR):
        if place < 2 * NEAR:
            side, k = (core, 1 - core)[place // NEAR], place % NEAR
            piece = pair_ref[side, width * k : width * k + width]
        else:
            piece = (far_ref, far_other_ref)[place - 2 * NEAR][...]
        product = lax.dot_general(
            piece, scaled, (((1,), (1,)), ((), ())), preferred_element_type=jnp.float32
        )
        block = piece_index(place)
        for q in range(4):
            part = product[40 * q : 40 * q + 40]
            rest = part[:, LANES:]
            first = jnp.concatenate([rest[8 * k : 8 * k + 8] for k in range(4)], axis=1)
            second = jnp.concatenate([rest[32:40], stats], axis=1)
            out_ref[4 * block + q] = jnp.concatenate([part[:, :LANES], first, second], axis=0).astype(
                jnp.bfloat16
            )


def finish_kernel(recv_ref, grad_ref, stats_ref):
    total = jnp.sum(recv_ref[...].astype(jnp.float32), axis=0)
    first, second = total[40:48], total[48:56]
    lane = lax.broadcasted_iota(jnp.int32, (1, LANES), 1)
    row = second[0:1]

    def pick(k):
        mine = (lane == 32 + k) | (lane == 36 + k) | (lane == 40 + k)
        return jnp.sum(jnp.where(mine, row, 0.0), axis=1, keepdims=True)

    divisor = jnp.maximum(pick(0), 1.0)
    rest = jnp.concatenate([first[:, 32 * k : 32 * k + 32] for k in range(4)] + [second[:, :32]], axis=0)
    grad_ref[...] = jnp.concatenate([total[:40], rest], axis=1) / divisor
    stats_ref[...] = (
        jnp.where(lane == 0, -pick(3), jnp.where(lane == 1, pick(1), jnp.where(lane == 2, pick(2), 0.0)))
        / divisor
    )


def body(
    attn_output, readout_vectors, w_out, log_gap, magnitude, reward_sign, keep_mask, move_plan
):
    local_rows, width = attn_output.shape
    attn_t, readout_t = attn_output.T, readout_vectors.T
    up, down, cross = [], [], []
    cores = [[2 * z, 2 * z + 1] for z in range(N_Z)]
    for z in range(N_Z):
        for c in range(2):
            up.append((2 * z + c, 2 * ((z + 1) % N_Z) + c))
            down.append((2 * ((z + 1) % N_Z) + c, 2 * z + c))
            cross.append((2 * ((z + 1) % N_Z) + 1 - c, 2 * z + c))
    rising, falling, nearby = readout_t, readout_t, [readout_t]
    for _ in range(3):
        rising = lax.ppermute(rising, "tensor", up)
        falling = lax.ppermute(falling, "tensor", down)
        nearby += [rising, falling]
    far_mine = lax.ppermute(rising, "tensor", up)
    far_other = lax.ppermute(falling, "tensor", cross)

    params = pltpu.CompilerParams(vmem_limit_bytes=24 << 20)
    tiled = (local_rows // LANES, LANES)
    w_blocks, aux, sums = pl.pallas_call(
        prepare_kernel,
        in_specs=[vmem_spec()] * 6,
        out_specs=[vmem_spec()] * 3,
        out_shape=[
            jax.ShapeDtypeStruct((N_TENSOR, width, width), w_out.dtype),
            jax.ShapeDtypeStruct((3, 8, LANES), jnp.float32),
            jax.ShapeDtypeStruct((8, LANES), jnp.float32),
        ],
        compiler_params=params,
    )(
        w_out,
        log_gap.astype(jnp.float32).reshape(tiled),
        magnitude.astype(jnp.float32).reshape(tiled),
        reward_sign.reshape(tiled),
        keep_mask.reshape(tiled),
        move_plan,
    )
    first, mine = pl.pallas_call(
        first_kernel,
        in_specs=[vmem_spec()] * (1 + NEAR),
        out_specs=[vmem_spec()] * 2,
        out_shape=[
            jax.ShapeDtypeStruct((width, local_rows), jnp.float32),
            jax.ShapeDtypeStruct((2, NEAR * width, local_rows), readout_t.dtype),
        ],
        compiler_params=params,
    )(w_blocks, *nearby)
    pair = lax.all_to_all(mine, "tensor", 0, 0, tiled=True, axis_index_groups=cores)
    partial_shift = pl.pallas_call(
        shift_kernel,
        in_specs=[vmem_spec()] * 6,
        out_specs=vmem_spec(),
        out_shape=jax.ShapeDtypeStruct((N_TENSOR, 8, LANES), jnp.float32),
        compiler_params=params,
    )(w_blocks, attn_t, first, pair, far_mine, far_other)
    shifts = lax.all_to_all(partial_shift, "tensor", 0, 0, tiled=True)
    chunks = pl.pallas_call(
        grad_kernel,
        in_specs=[vmem_spec()] * 7,
        out_specs=vmem_spec(),
        out_shape=jax.ShapeDtypeStruct((N_DP, CHUNK_ROWS, LANES), jnp.bfloat16),
        compiler_params=params,
    )(shifts, aux, sums, attn_t, pair, far_mine, far_other)
    received = lax.all_to_all(chunks, "dp", 0, 0, tiled=True)
    grad_t, stats = pl.pallas_call(
        finish_kernel,
        in_specs=[vmem_spec()],
        out_specs=[vmem_spec(), vmem_spec()],
        out_shape=[
            jax.ShapeDtypeStruct((40, width), jnp.float32),
            jax.ShapeDtypeStruct((1, LANES), jnp.float32),
        ],
        compiler_params=pltpu.CompilerParams(vmem_limit_bytes=24 << 20),
    )(received)
    return grad_t.T, stats[0, :3]


def solution(mesh):
    placed = (
        P("dp", "tensor"),
        P("dp", "tensor"),
        P("tensor", None),
        P("dp"),
        P("dp"),
        P("dp"),
        P("dp"),
        P(),
    )
    return jax.shard_map(
        body, mesh=mesh, in_specs=placed, out_specs=(P("tensor", "dp"), P()), check_vma=False
    )
```

```python
import jax
import jax.numpy as jnp
from jax import lax
from jax.experimental import pallas as pl
from jax.experimental.pallas import tpu as pltpu
from jax.sharding import PartitionSpec as P

EPS_LOW = 0.2
EPS_HIGH = 0.28
LOSS_SCALE = 16384.0
N_DP = 64
N_TENSOR = 16
CHUNK_ROWS = 56
LANES = 128
QUAD = 4


def vmem_spec():
    return pl.BlockSpec(memory_space=pltpu.VMEM)


def split_kernel(w_ref, keep_ref, send_ref):
    width = w_ref.shape[0]
    chip = (lax.axis_index("tensor") >> 1) & 1
    for place in range(QUAD):
        columns = [w_ref[:, width * (QUAD * k + place) :][:, :width] for k in range(QUAD)]
        part = jnp.concatenate(columns, axis=1)

        @pl.when(chip == place // 2)
        def _():
            keep_ref[place % 2] = part

        @pl.when(chip != place // 2)
        def _():
            send_ref[place % 2] = part


def shift_kernel(w_ref, attn_ref, readout_ref, out_ref):
    width = w_ref.shape[1] // 2
    chip = (lax.axis_index("tensor") >> 1) & 1
    readout = readout_ref[...]
    row = None
    for place in range(QUAD):
        start = pl.multiple_of((chip ^ (place // 2)) * width, width)
        projected = jnp.dot(
            w_ref[place % 2, pl.ds(start, width)], readout, preferred_element_type=jnp.float32
        )
        attn = attn_ref[width * place : width * place + width].astype(jnp.float32)
        part = jnp.sum(projected * attn, axis=0, keepdims=True)
        row = part if row is None else row + part
    rows = [row[:, LANES * r : LANES * r + LANES] for r in range(6)]
    block = jnp.concatenate(rows + [jnp.zeros((2, LANES), jnp.float32)], axis=0)
    for k in range(N_TENSOR):
        out_ref[k] = block


def weight_kernel(gap_ref, size_ref, sign_ref, keep_ref, plan_ref, aux_ref, sums_ref):
    owner = lax.broadcasted_iota(jnp.int32, plan_ref.shape, 0)
    live_total = jnp.sum(jnp.where(owner == lax.axis_index("dp"), plan_ref[...], 0))
    shape = gap_ref.shape
    slot_ids = lax.broadcasted_iota(jnp.int32, shape, 0) * LANES + lax.broadcasted_iota(jnp.int32, shape, 1)
    weight = jnp.where(slot_ids < live_total, keep_ref[...], 0).astype(jnp.float32)
    gap = gap_ref[...]
    advantage = (2 * sign_ref[...] - 1).astype(jnp.float32) * size_ref[...]
    base_ratio = jnp.exp(gap)
    clip_high = jnp.where((advantage > 0) & (base_ratio > 1.0 + EPS_HIGH), 1.0, 0.0)
    clip_low = jnp.where((advantage < 0) & (base_ratio < 1.0 - EPS_LOW), 1.0, 0.0)
    signed = weight * advantage
    zeros = jnp.zeros((2, LANES), jnp.float32)
    base = -LOSS_SCALE * signed * (1.0 - clip_high - clip_low)
    for k, value in enumerate((gap, signed, base)):
        aux_ref[k] = jnp.concatenate([value, zeros], axis=0)
    lane = lax.broadcasted_iota(jnp.int32, (8, LANES), 1)
    which = jnp.where((lane >= 32) & (lane < 44), lane & 3, 3)
    count, high, low = jnp.sum(weight), jnp.sum(weight * clip_high), jnp.sum(weight * clip_low)
    sums_ref[...] = jnp.where(
        which == 0, count, jnp.where(which == 1, high, jnp.where(which == 2, low, 0.0))
    )


def grad_kernel(recv_ref, aux_ref, sums_ref, attn_ref, readout_ref, out_ref):
    width = attn_ref.shape[0] // QUAD
    shift = jnp.sum(recv_ref[...], axis=0)
    gap, signed, base = aux_ref[0], aux_ref[1], aux_ref[2]
    ratio = jnp.exp(gap + shift)
    loss = jnp.sum(
        jnp.minimum(ratio * signed, jnp.clip(ratio, 1.0 - EPS_LOW, 1.0 + EPS_HIGH) * signed)
    )
    coefficient = base * ratio
    row = jnp.concatenate([coefficient[r : r + 1] for r in range(6)], axis=1)
    scaled = (attn_ref[...].astype(jnp.float32) * row).astype(jnp.bfloat16)
    lane = lax.broadcasted_iota(jnp.int32, (8, LANES), 1)
    is_loss = (lane == 35) | (lane == 39) | (lane == 43)
    value = jnp.where(is_loss, loss, sums_ref[...])
    high = value.astype(jnp.bfloat16).astype(jnp.float32)
    middle = (value - high).astype(jnp.bfloat16).astype(jnp.float32)
    low = value - high - middle
    stats = jnp.where(lane < 36, high, jnp.where(lane < 40, middle, low))[:, 32:]
    for place in range(QUAD):
        mine = scaled[width * place : width * place + width]
        for k in range(QUAD):
            product = lax.dot_general(
                readout_ref[width * k : width * k + width],
                mine,
                (((1,), (1,)), ((), ())),
                preferred_element_type=jnp.float32,
            )
            for q in range(4):
                part = product[40 * q : 40 * q + 40]
                rest = part[:, LANES:]
                first = jnp.concatenate([rest[8 * r : 8 * r + 8] for r in range(4)], axis=1)
                second = jnp.concatenate([rest[32:40], stats], axis=1)
                out_ref[16 * k + 4 * place + q] = jnp.concatenate(
                    [part[:, :LANES], first, second], axis=0
                ).astype(jnp.bfloat16)


def finish_kernel(recv_ref, grad_ref, stats_ref):
    total = jnp.sum(recv_ref[...].astype(jnp.float32), axis=0)
    first, second = total[40:48], total[48:56]
    lane = lax.broadcasted_iota(jnp.int32, (1, LANES), 1)
    row = second[0:1]

    def pick(k):
        mine = (lane == 32 + k) | (lane == 36 + k) | (lane == 40 + k)
        return jnp.sum(jnp.where(mine, row, 0.0), axis=1, keepdims=True)

    divisor = jnp.maximum(pick(0), 1.0)
    rest = jnp.concatenate([first[:, 32 * k : 32 * k + 32] for k in range(4)] + [second[:, :32]], axis=0)
    grad_ref[...] = jnp.concatenate([total[:40], rest], axis=1) / divisor
    stats_ref[...] = (
        jnp.where(lane == 0, -pick(3), jnp.where(lane == 1, pick(1), jnp.where(lane == 2, pick(2), 0.0)))
        / divisor
    )


def body(
    attn_output, readout_vectors, w_out, log_gap, magnitude, reward_sign, keep_mask, move_plan
):
    local_rows, width = attn_output.shape
    attn_t, readout_t = attn_output.T, readout_vectors.T
    params = pltpu.CompilerParams(vmem_limit_bytes=24 << 20)
    quads = [[QUAD * q + p for p in range(QUAD)] for q in range(QUAD)]
    strided = [[QUAD * q + p for q in range(QUAD)] for p in range(QUAD)]
    cores = [[2 * z, 2 * z + 1] for z in range(N_TENSOR // 2)]

    columns = jax.ShapeDtypeStruct((2, width, QUAD * width), w_out.dtype)
    kept, sent = pl.pallas_call(
        split_kernel,
        in_specs=[vmem_spec()],
        out_specs=[vmem_spec()] * 2,
        out_shape=[columns] * 2,
        compiler_params=params,
    )(w_out)
    got = lax.ppermute(sent, "tensor", [(t, t ^ 2) for t in range(N_TENSOR)])
    attn_all = lax.all_gather(attn_t, "tensor", axis=0, tiled=True, axis_index_groups=quads)
    readout_all = lax.all_gather(readout_t, "tensor", axis=0, tiled=True, axis_index_groups=strided)
    weights = lax.all_to_all(
        jnp.concatenate([kept, got], axis=1), "tensor", 0, 0, tiled=True, axis_index_groups=cores
    )
    partial_shift = pl.pallas_call(
        shift_kernel,
        in_specs=[vmem_spec()] * 3,
        out_specs=vmem_spec(),
        out_shape=jax.ShapeDtypeStruct((N_TENSOR, 8, LANES), jnp.float32),
        compiler_params=params,
    )(weights, attn_all, readout_all)
    shifts = lax.all_to_all(partial_shift, "tensor", 0, 0, tiled=True)

    tiled = (local_rows // LANES, LANES)
    aux, sums = pl.pallas_call(
        weight_kernel,
        in_specs=[vmem_spec()] * 5,
        out_specs=[vmem_spec()] * 2,
        out_shape=[
            jax.ShapeDtypeStruct((3, 8, LANES), jnp.float32),
            jax.ShapeDtypeStruct((8, LANES), jnp.float32),
        ],
        compiler_params=params,
    )(
        log_gap.astype(jnp.float32).reshape(tiled),
        magnitude.astype(jnp.float32).reshape(tiled),
        reward_sign.reshape(tiled),
        keep_mask.reshape(tiled),
        move_plan,
    )
    chunks = pl.pallas_call(
        grad_kernel,
        in_specs=[vmem_spec()] * 5,
        out_specs=vmem_spec(),
        out_shape=jax.ShapeDtypeStruct((N_DP, CHUNK_ROWS, LANES), jnp.bfloat16),
        compiler_params=params,
    )(shifts, aux, sums, attn_all, readout_all)
    received = lax.all_to_all(chunks, "dp", 0, 0, tiled=True)
    grad_t, stats = pl.pallas_call(
        finish_kernel,
        in_specs=[vmem_spec()],
        out_specs=[vmem_spec(), vmem_spec()],
        out_shape=[
            jax.ShapeDtypeStruct((40, width), jnp.float32),
            jax.ShapeDtypeStruct((1, LANES), jnp.float32),
        ],
        compiler_params=params,
    )(received)
    homes = []
    for m in range(N_DP):
        for t in range(N_TENSOR):
            low, high = t % QUAD, m // 4 % QUAD
            homes.append((N_TENSOR * m + t, N_TENSOR * (m + 4 * (low - high)) + t + high - low))
    grad_t = lax.ppermute(grad_t, ("dp", "tensor"), homes)
    return grad_t.T, stats[0, :3]


def solution(mesh):
    placed = (
        P("dp", "tensor"),
        P("dp", "tensor"),
        P("tensor", None),
        P("dp"),
        P("dp"),
        P("dp"),
        P("dp"),
        P(),
    )
    return jax.shard_map(
        body, mesh=mesh, in_specs=placed, out_specs=(P("tensor", "dp"), P()), check_vma=False
    )
```

```python
import jax
import jax.numpy as jnp
from jax import lax
from jax.experimental import pallas as pl
from jax.experimental.pallas import tpu as pltpu
from jax.sharding import PartitionSpec as P

EPS_LOW = 0.2
EPS_HIGH = 0.28
LOSS_SCALE = 16384.0
N_DP = 64
N_TENSOR = 16
CHUNK_ROWS = 56
LANES = 128
N_Z = 8
STEPS = (0, -1, 1, -2, 2, -3, 3, 4)


def vmem_spec():
    return pl.BlockSpec(memory_space=pltpu.VMEM)


def piece_index(place):
    device = lax.axis_index("tensor")
    side = (device & 1) ^ (place // N_Z)
    return (((device >> 1) + N_Z + STEPS[place % N_Z]) & (N_Z - 1)) * 2 + side


def prepare_kernel(w_ref, gap_ref, size_ref, sign_ref, keep_ref, plan_ref, out_ref, aux_ref, sums_ref):
    width = out_ref.shape[2]
    for k in range(N_TENSOR):
        out_ref[k] = w_ref[:, width * k : width * k + width]
    owner = lax.broadcasted_iota(jnp.int32, plan_ref.shape, 0)
    live_total = jnp.sum(jnp.where(owner == lax.axis_index("dp"), plan_ref[...], 0))
    shape = gap_ref.shape
    slot_ids = lax.broadcasted_iota(jnp.int32, shape, 0) * LANES + lax.broadcasted_iota(jnp.int32, shape, 1)
    weight = jnp.where(slot_ids < live_total, keep_ref[...], 0).astype(jnp.float32)
    gap = gap_ref[...]
    advantage = (2 * sign_ref[...] - 1).astype(jnp.float32) * size_ref[...]
    base_ratio = jnp.exp(gap)
    clip_high = jnp.where((advantage > 0) & (base_ratio > 1.0 + EPS_HIGH), 1.0, 0.0)
    clip_low = jnp.where((advantage < 0) & (base_ratio < 1.0 - EPS_LOW), 1.0, 0.0)
    signed = weight * advantage
    zeros = jnp.zeros((2, LANES), jnp.float32)
    base = -LOSS_SCALE * signed * (1.0 - clip_high - clip_low)
    for k, value in enumerate((gap, signed, base)):
        aux_ref[k] = jnp.concatenate([value, zeros], axis=0)
    lane = lax.broadcasted_iota(jnp.int32, (8, LANES), 1)
    which = jnp.where((lane >= 32) & (lane < 44), lane & 3, 3)
    count, high, low = jnp.sum(weight), jnp.sum(weight * clip_high), jnp.sum(weight * clip_low)
    sums_ref[...] = jnp.where(
        which == 0, count, jnp.where(which == 1, high, jnp.where(which == 2, low, 0.0))
    )


def project(w_ref, places, pieces):
    total = None
    for place, piece in zip(places, pieces):
        product = jnp.dot(w_ref[piece_index(place)], piece, preferred_element_type=jnp.float32)
        total = product if total is None else total + product
    return total


def first_kernel(w_ref, *refs):
    piece_refs, (out_ref, mine_ref) = refs[:N_Z], refs[N_Z:]
    width = w_ref.shape[1]
    pieces = [piece_ref[...] for piece_ref in piece_refs]
    for k, piece in enumerate(pieces):
        mine_ref[width * k : width * k + width] = piece
    out_ref[...] = project(w_ref, range(N_Z), pieces)


def shift_kernel(w_ref, attn_ref, first_ref, other_ref, out_ref):
    width = w_ref.shape[1]
    pieces = [other_ref[width * k : width * k + width] for k in range(N_Z)]
    total = first_ref[...] + project(w_ref, range(N_Z, N_TENSOR), pieces)
    row = jnp.sum(total * attn_ref[...].astype(jnp.float32), axis=0, keepdims=True)
    rows = [row[:, LANES * r : LANES * r + LANES] for r in range(6)]
    block = jnp.concatenate(rows + [jnp.zeros((2, LANES), jnp.float32)], axis=0)
    for k in range(N_TENSOR):
        out_ref[k] = block


def grad_kernel(
    recv_ref,
    aux_ref,
    sums_ref,
    attn_ref,
    mine_ref,
    other_ref,
    out_ref,
):
    width = attn_ref.shape[0]
    shift = jnp.sum(recv_ref[...], axis=0)
    gap, signed, base = aux_ref[0], aux_ref[1], aux_ref[2]
    ratio = jnp.exp(gap + shift)
    loss = jnp.sum(
        jnp.minimum(ratio * signed, jnp.clip(ratio, 1.0 - EPS_LOW, 1.0 + EPS_HIGH) * signed)
    )
    coefficient = base * ratio
    row = jnp.concatenate([coefficient[r : r + 1] for r in range(6)], axis=1)
    scaled = (attn_ref[...].astype(jnp.float32) * row).astype(jnp.bfloat16)
    lane = lax.broadcasted_iota(jnp.int32, (8, LANES), 1)
    is_loss = (lane == 35) | (lane == 39) | (lane == 43)
    value = jnp.where(is_loss, loss, sums_ref[...])
    high = value.astype(jnp.bfloat16).astype(jnp.float32)
    middle = (value - high).astype(jnp.bfloat16).astype(jnp.float32)
    low = value - high - middle
    stats = jnp.where(lane < 36, high, jnp.where(lane < 40, middle, low))[:, 32:]
    for place in range(N_TENSOR):
        k = place % N_Z
        piece = (mine_ref, other_ref)[place // N_Z][width * k : width * k + width]
        product = lax.dot_general(
            piece, scaled, (((1,), (1,)), ((), ())), preferred_element_type=jnp.float32
        )
        block = piece_index(place)
        for q in range(4):
            part = product[40 * q : 40 * q + 40]
            rest = part[:, LANES:]
            first = jnp.concatenate([rest[8 * k : 8 * k + 8] for k in range(4)], axis=1)
            second = jnp.concatenate([rest[32:40], stats], axis=1)
            out_ref[4 * block + q] = jnp.concatenate([part[:, :LANES], first, second], axis=0).astype(
                jnp.bfloat16
            )


def finish_kernel(recv_ref, grad_ref, stats_ref):
    total = jnp.sum(recv_ref[...].astype(jnp.float32), axis=0)
    first, second = total[40:48], total[48:56]
    lane = lax.broadcasted_iota(jnp.int32, (1, LANES), 1)
    row = second[0:1]

    def pick(k):
        mine = (lane == 32 + k) | (lane == 36 + k) | (lane == 40 + k)
        return jnp.sum(jnp.where(mine, row, 0.0), axis=1, keepdims=True)

    divisor = jnp.maximum(pick(0), 1.0)
    rest = jnp.concatenate([first[:, 32 * k : 32 * k + 32] for k in range(4)] + [second[:, :32]], axis=0)
    grad_ref[...] = jnp.concatenate([total[:40], rest], axis=1) / divisor
    stats_ref[...] = (
        jnp.where(lane == 0, -pick(3), jnp.where(lane == 1, pick(1), jnp.where(lane == 2, pick(2), 0.0)))
        / divisor
    )


def body(
    attn_output, readout_vectors, w_out, log_gap, magnitude, reward_sign, keep_mask, move_plan
):
    local_rows, width = attn_output.shape
    attn_t, readout_t = attn_output.T, readout_vectors.T
    up, down, swap = [], [], []
    for z in range(N_Z):
        for c in range(2):
            up.append((2 * z + c, 2 * ((z + 1) % N_Z) + c))
            down.append((2 * ((z + 1) % N_Z) + c, 2 * z + c))
            swap.append((2 * z + 1 - c, 2 * z + c))
    rising, falling, nearby = readout_t, readout_t, [readout_t]
    for _ in range(3):
        rising = lax.ppermute(rising, "tensor", up)
        falling = lax.ppermute(falling, "tensor", down)
        nearby += [rising, falling]
    nearby.append(lax.ppermute(rising, "tensor", up))

    params = pltpu.CompilerParams(vmem_limit_bytes=24 << 20)
    tiled = (local_rows // LANES, LANES)
    w_blocks, aux, sums = pl.pallas_call(
        prepare_kernel,
        in_specs=[vmem_spec()] * 6,
        out_specs=[vmem_spec()] * 3,
        out_shape=[
            jax.ShapeDtypeStruct((N_TENSOR, width, width), w_out.dtype),
            jax.ShapeDtypeStruct((3, 8, LANES), jnp.float32),
            jax.ShapeDtypeStruct((8, LANES), jnp.float32),
        ],
        compiler_params=params,
    )(
        w_out,
        log_gap.astype(jnp.float32).reshape(tiled),
        magnitude.astype(jnp.float32).reshape(tiled),
        reward_sign.reshape(tiled),
        keep_mask.reshape(tiled),
        move_plan,
    )
    first, mine = pl.pallas_call(
        first_kernel,
        in_specs=[vmem_spec()] * (1 + N_Z),
        out_specs=[vmem_spec()] * 2,
        out_shape=[
            jax.ShapeDtypeStruct((width, local_rows), jnp.float32),
            jax.ShapeDtypeStruct((N_Z * width, local_rows), readout_t.dtype),
        ],
        compiler_params=params,
    )(w_blocks, *nearby)
    other = lax.ppermute(mine, "tensor", swap)
    partial_shift = pl.pallas_call(
        shift_kernel,
        in_specs=[vmem_spec()] * 4,
        out_specs=vmem_spec(),
        out_shape=jax.ShapeDtypeStruct((N_TENSOR, 8, LANES), jnp.float32),
        compiler_params=params,
    )(w_blocks, attn_t, first, other)
    shifts = lax.all_to_all(partial_shift, "tensor", 0, 0, tiled=True)
    chunks = pl.pallas_call(
        grad_kernel,
        in_specs=[vmem_spec()] * 6,
        out_specs=vmem_spec(),
        out_shape=jax.ShapeDtypeStruct((N_DP, CHUNK_ROWS, LANES), jnp.bfloat16),
        compiler_params=params,
    )(shifts, aux, sums, attn_t, mine, other)
    received = lax.all_to_all(chunks, "dp", 0, 0, tiled=True)
    grad_t, stats = pl.pallas_call(
        finish_kernel,
        in_specs=[vmem_spec()],
        out_specs=[vmem_spec(), vmem_spec()],
        out_shape=[
            jax.ShapeDtypeStruct((40, width), jnp.float32),
            jax.ShapeDtypeStruct((1, LANES), jnp.float32),
        ],
        compiler_params=pltpu.CompilerParams(vmem_limit_bytes=24 << 20),
    )(received)
    return grad_t.T, stats[0, :3]


def solution(mesh):
    placed = (
        P("dp", "tensor"),
        P("dp", "tensor"),
        P("tensor", None),
        P("dp"),
        P("dp"),
        P("dp"),
        P("dp"),
        P(),
    )
    return jax.shard_map(
        body, mesh=mesh, in_specs=placed, out_specs=(P("tensor", "dp"), P()), check_vma=False
    )
```

```python
import jax
import jax.numpy as jnp
from jax import lax
from jax.experimental import pallas as pl
from jax.experimental.pallas import tpu as pltpu
from jax.sharding import PartitionSpec as P

EPS_LOW = 0.2
EPS_HIGH = 0.28
LOSS_SCALE = 16384.0
N_TENSOR = 16
LINE_ROWS = 408
CHUNK_ROWS = 56
LANES = 128
N_Z = 8
STEPS = (0, -1, 1, -2, 2, -3, 3, 4)


def vmem_spec():
    return pl.BlockSpec(memory_space=pltpu.VMEM)


def piece_index(place):
    device = lax.axis_index("tensor")
    side = (device & 1) ^ (place // N_Z)
    return (((device >> 1) + N_Z + STEPS[place % N_Z]) & (N_Z - 1)) * 2 + side


def prepare_kernel(w_ref, gap_ref, size_ref, sign_ref, keep_ref, plan_ref, out_ref, aux_ref, sums_ref):
    width = out_ref.shape[2]
    for k in range(N_TENSOR):
        out_ref[k] = w_ref[:, width * k : width * k + width]
    owner = lax.broadcasted_iota(jnp.int32, plan_ref.shape, 0)
    live_total = jnp.sum(jnp.where(owner == lax.axis_index("dp"), plan_ref[...], 0))
    shape = gap_ref.shape
    slot_ids = lax.broadcasted_iota(jnp.int32, shape, 0) * LANES + lax.broadcasted_iota(jnp.int32, shape, 1)
    weight = jnp.where(slot_ids < live_total, keep_ref[...], 0).astype(jnp.float32)
    gap = gap_ref[...]
    advantage = (2 * sign_ref[...] - 1).astype(jnp.float32) * size_ref[...]
    base_ratio = jnp.exp(gap)
    clip_high = jnp.where((advantage > 0) & (base_ratio > 1.0 + EPS_HIGH), 1.0, 0.0)
    clip_low = jnp.where((advantage < 0) & (base_ratio < 1.0 - EPS_LOW), 1.0, 0.0)
    signed = weight * advantage
    zeros = jnp.zeros((2, LANES), jnp.float32)
    base = -LOSS_SCALE * signed * (1.0 - clip_high - clip_low)
    for k, value in enumerate((gap, signed, base)):
        aux_ref[k] = jnp.concatenate([value, zeros], axis=0)
    lane = lax.broadcasted_iota(jnp.int32, (8, LANES), 1)
    which = jnp.where((lane >= 32) & (lane < 44), lane & 3, 3)
    count, high, low = jnp.sum(weight), jnp.sum(weight * clip_high), jnp.sum(weight * clip_low)
    sums_ref[...] = jnp.where(
        which == 0, count, jnp.where(which == 1, high, jnp.where(which == 2, low, 0.0))
    )


def project(w_ref, places, pieces):
    total = None
    for place, piece in zip(places, pieces):
        product = jnp.dot(w_ref[piece_index(place)], piece, preferred_element_type=jnp.float32)
        total = product if total is None else total + product
    return total


def first_kernel(w_ref, *refs):
    piece_refs, (out_ref, mine_ref) = refs[:N_Z], refs[N_Z:]
    width = w_ref.shape[1]
    pieces = [piece_ref[...] for piece_ref in piece_refs]
    for k, piece in enumerate(pieces):
        mine_ref[width * k : width * k + width] = piece
    out_ref[...] = project(w_ref, range(N_Z), pieces)


def shift_kernel(w_ref, attn_ref, first_ref, other_ref, out_ref):
    width = w_ref.shape[1]
    pieces = [other_ref[width * k : width * k + width] for k in range(N_Z)]
    total = first_ref[...] + project(w_ref, range(N_Z, N_TENSOR), pieces)
    row = jnp.sum(total * attn_ref[...].astype(jnp.float32), axis=0, keepdims=True)
    rows = [row[:, LANES * r : LANES * r + LANES] for r in range(6)]
    block = jnp.concatenate(rows + [jnp.zeros((2, LANES), jnp.float32)], axis=0)
    for k in range(N_TENSOR):
        out_ref[k] = block


def in_three(value, lane):
    high = value.astype(jnp.bfloat16).astype(jnp.float32)
    middle = (value - high).astype(jnp.bfloat16).astype(jnp.float32)
    low = value - high - middle
    return jnp.where(lane < 36, high, jnp.where(lane < 40, middle, low))


def pick(row, lane, k):
    mine = (lane == 32 + k) | (lane == 36 + k) | (lane == 40 + k)
    return jnp.sum(jnp.where(mine, row, 0.0), axis=1, keepdims=True)


def slot(k, g):
    place = 5 * k + g
    return 320 + 8 * (place // 4), 32 * (place % 4)


def grad_kernel(
    recv_ref,
    aux_ref,
    sums_ref,
    attn_ref,
    mine_ref,
    other_ref,
    out_ref,
    wide_ref,
):
    width = attn_ref.shape[0]
    shift = jnp.sum(recv_ref[...], axis=0)
    gap, signed, base = aux_ref[0], aux_ref[1], aux_ref[2]
    ratio = jnp.exp(gap + shift)
    loss = jnp.sum(
        jnp.minimum(ratio * signed, jnp.clip(ratio, 1.0 - EPS_LOW, 1.0 + EPS_HIGH) * signed)
    )
    coefficient = base * ratio
    row = jnp.concatenate([coefficient[r : r + 1] for r in range(6)], axis=1)
    scaled = (attn_ref[...].astype(jnp.float32) * row).astype(jnp.bfloat16)
    lane = lax.broadcasted_iota(jnp.int32, (8, LANES), 1)
    is_loss = (lane == 35) | (lane == 39) | (lane == 43)
    value = jnp.where(is_loss, loss, sums_ref[...])
    wide_ref[:, LINE_ROWS - 8 :] = jnp.broadcast_to(in_three(value, lane)[None], (8, 8, LANES))
    core = lax.axis_index("tensor") & 1
    for place in range(N_TENSOR):
        k = place % N_Z
        piece = (mine_ref, other_ref)[place // N_Z][width * k : width * k + width]
        product = lax.dot_general(
            piece, scaled, (((1,), (1,)), ((), ())), preferred_element_type=jnp.float32
        )
        side = core ^ (place // N_Z)
        for q in range(4):
            part = product[40 * q : 40 * q + 40]
            wide_ref[4 * side + q, 40 * k : 40 * k + 40] = part[:, :LANES]
            for g in range(5):
                row, column = slot(k, g)
                wide_ref[4 * side + q, row : row + 8, column : column + 32] = part[
                    8 * g : 8 * g + 8, LANES:
                ]
    out_ref[...] = wide_ref[...].astype(jnp.bfloat16)


def line_kernel(recv_ref, out_ref):
    total = jnp.sum(recv_ref[...].astype(jnp.float32), axis=0)
    lane = lax.broadcasted_iota(jnp.int32, (8, LANES), 1)
    row = total[LINE_ROWS - 8 :]
    value = jnp.where((lane >= 32) & (lane < 44), pick(row, lane, 3), 0.0)
    for k in range(3):
        value = jnp.where((lane >= 32) & (lane < 44) & ((lane & 3) == k), pick(row, lane, k), value)
    stats = in_three(value, lane)[:, 32:]
    place_z = lax.axis_index("tensor") >> 1
    for k in range(N_Z):
        parts = []
        for g in range(5):
            row, column = slot(k, g)
            parts.append(total[row : row + 8, column : column + 32])
        chunk = [
            total[40 * k : 40 * k + 40],
            jnp.concatenate(parts[:4], axis=1),
            jnp.concatenate([parts[4], stats], axis=1),
        ]
        out_ref[(place_z + N_Z + STEPS[k]) & (N_Z - 1)] = jnp.concatenate(chunk, axis=0).astype(
            jnp.bfloat16
        )


def finish_kernel(recv_ref, grad_ref, stats_ref):
    total = jnp.sum(recv_ref[...].astype(jnp.float32), axis=0)
    first, second = total[40:48], total[48:56]
    lane = lax.broadcasted_iota(jnp.int32, (1, LANES), 1)
    row = second[0:1]

    divisor = jnp.maximum(pick(row, lane, 0), 1.0)
    rest = jnp.concatenate([first[:, 32 * k : 32 * k + 32] for k in range(4)] + [second[:, :32]], axis=0)
    grad_ref[...] = jnp.concatenate([total[:40], rest], axis=1) / divisor
    stats_ref[...] = (
        jnp.where(lane == 0, -pick(row, lane, 3), jnp.where(lane == 1, pick(row, lane, 1), jnp.where(lane == 2, pick(row, lane, 2), 0.0)))
        / divisor
    )


def body(
    attn_output, readout_vectors, w_out, log_gap, magnitude, reward_sign, keep_mask, move_plan
):
    local_rows, width = attn_output.shape
    attn_t, readout_t = attn_output.T, readout_vectors.T
    up, down, swap = [], [], []
    for z in range(N_Z):
        for c in range(2):
            up.append((2 * z + c, 2 * ((z + 1) % N_Z) + c))
            down.append((2 * ((z + 1) % N_Z) + c, 2 * z + c))
            swap.append((2 * z + 1 - c, 2 * z + c))
    rising, falling, nearby = readout_t, readout_t, [readout_t]
    for _ in range(3):
        rising = lax.ppermute(rising, "tensor", up)
        falling = lax.ppermute(falling, "tensor", down)
        nearby += [rising, falling]
    nearby.append(lax.ppermute(rising, "tensor", up))

    params = pltpu.CompilerParams(vmem_limit_bytes=24 << 20)
    tiled = (local_rows // LANES, LANES)
    w_blocks, aux, sums = pl.pallas_call(
        prepare_kernel,
        in_specs=[vmem_spec()] * 6,
        out_specs=[vmem_spec()] * 3,
        out_shape=[
            jax.ShapeDtypeStruct((N_TENSOR, width, width), w_out.dtype),
            jax.ShapeDtypeStruct((3, 8, LANES), jnp.float32),
            jax.ShapeDtypeStruct((8, LANES), jnp.float32),
        ],
        compiler_params=params,
    )(
        w_out,
        log_gap.astype(jnp.float32).reshape(tiled),
        magnitude.astype(jnp.float32).reshape(tiled),
        reward_sign.reshape(tiled),
        keep_mask.reshape(tiled),
        move_plan,
    )
    first, mine = pl.pallas_call(
        first_kernel,
        in_specs=[vmem_spec()] * (1 + N_Z),
        out_specs=[vmem_spec()] * 2,
        out_shape=[
            jax.ShapeDtypeStruct((width, local_rows), jnp.float32),
            jax.ShapeDtypeStruct((N_Z * width, local_rows), readout_t.dtype),
        ],
        compiler_params=params,
    )(w_blocks, *nearby)
    other = lax.ppermute(mine, "tensor", swap)
    partial_shift = pl.pallas_call(
        shift_kernel,
        in_specs=[vmem_spec()] * 4,
        out_specs=vmem_spec(),
        out_shape=jax.ShapeDtypeStruct((N_TENSOR, 8, LANES), jnp.float32),
        compiler_params=params,
    )(w_blocks, attn_t, first, other)
    shifts = lax.all_to_all(partial_shift, "tensor", 0, 0, tiled=True)
    chunks = pl.pallas_call(
        grad_kernel,
        in_specs=[vmem_spec()] * 6,
        out_specs=vmem_spec(),
        out_shape=jax.ShapeDtypeStruct((8, LINE_ROWS, LANES), jnp.bfloat16),
        scratch_shapes=[pltpu.VMEM((8, LINE_ROWS, LANES), jnp.float32)],
        compiler_params=params,
    )(shifts, aux, sums, attn_t, mine, other)
    along_y = [[8 * x + y for y in range(8)] for x in range(8)]
    along_x = [[8 * x + y for x in range(8)] for y in range(8)]
    received = lax.all_to_all(chunks, "dp", 0, 0, tiled=True, axis_index_groups=along_y)
    chunks = pl.pallas_call(
        line_kernel,
        in_specs=[vmem_spec()],
        out_specs=vmem_spec(),
        out_shape=jax.ShapeDtypeStruct((8, CHUNK_ROWS, LANES), jnp.bfloat16),
        compiler_params=params,
    )(received)
    received = lax.all_to_all(chunks, "dp", 0, 0, tiled=True, axis_index_groups=along_x)
    grad_t, stats = pl.pallas_call(
        finish_kernel,
        in_specs=[vmem_spec()],
        out_specs=[vmem_spec(), vmem_spec()],
        out_shape=[
            jax.ShapeDtypeStruct((40, width), jnp.float32),
            jax.ShapeDtypeStruct((1, LANES), jnp.float32),
        ],
        compiler_params=pltpu.CompilerParams(vmem_limit_bytes=24 << 20),
    )(received)
    return grad_t.T, stats[0, :3]


def solution(mesh):
    placed = (
        P("dp", "tensor"),
        P("dp", "tensor"),
        P("tensor", None),
        P("dp"),
        P("dp"),
        P("dp"),
        P("dp"),
        P(),
    )
    return jax.shard_map(
        body, mesh=mesh, in_specs=placed, out_specs=(P("tensor", "dp"), P()), check_vma=False
    )
```

```python
import jax
import jax.numpy as jnp
from jax import lax
from jax.experimental import pallas as pl
from jax.experimental.pallas import tpu as pltpu
from jax.sharding import PartitionSpec as P

EPS_LOW = 0.2
EPS_HIGH = 0.28
LOSS_SCALE = 16384.0
N_DP = 64
N_TENSOR = 16
CHUNK_ROWS = 56
LANES = 128
N_Z = 8
STEPS = (0, -1, 1, -2, 2, -3, 3, 4)


def vmem_spec():
    return pl.BlockSpec(memory_space=pltpu.VMEM)


def piece_index(place):
    device = lax.axis_index("tensor")
    side = (device & 1) ^ (place // N_Z)
    step = (1 - 2 * side) * STEPS[place % N_Z]
    return (((device >> 1) + N_Z + step) & (N_Z - 1)) * 2 + side


def prepare_kernel(w_ref, gap_ref, size_ref, sign_ref, keep_ref, plan_ref, out_ref, aux_ref, sums_ref):
    width = out_ref.shape[2]
    for k in range(N_TENSOR):
        out_ref[k] = w_ref[:, width * k : width * k + width]
    owner = lax.broadcasted_iota(jnp.int32, plan_ref.shape, 0)
    live_total = jnp.sum(jnp.where(owner == lax.axis_index("dp"), plan_ref[...], 0))
    shape = gap_ref.shape
    slot_ids = lax.broadcasted_iota(jnp.int32, shape, 0) * LANES + lax.broadcasted_iota(jnp.int32, shape, 1)
    weight = jnp.where(slot_ids < live_total, keep_ref[...], 0).astype(jnp.float32)
    gap = gap_ref[...]
    advantage = (2 * sign_ref[...] - 1).astype(jnp.float32) * size_ref[...]
    base_ratio = jnp.exp(gap)
    clip_high = jnp.where((advantage > 0) & (base_ratio > 1.0 + EPS_HIGH), 1.0, 0.0)
    clip_low = jnp.where((advantage < 0) & (base_ratio < 1.0 - EPS_LOW), 1.0, 0.0)
    signed = weight * advantage
    zeros = jnp.zeros((2, LANES), jnp.float32)
    base = -LOSS_SCALE * signed * (1.0 - clip_high - clip_low)
    for k, value in enumerate((gap, signed, base)):
        aux_ref[k] = jnp.concatenate([value, zeros], axis=0)
    lane = lax.broadcasted_iota(jnp.int32, (8, LANES), 1)
    which = jnp.where((lane >= 32) & (lane < 44), lane & 3, 3)
    count, high, low = jnp.sum(weight), jnp.sum(weight * clip_high), jnp.sum(weight * clip_low)
    sums_ref[...] = jnp.where(
        which == 0, count, jnp.where(which == 1, high, jnp.where(which == 2, low, 0.0))
    )


def project(w_ref, places, pieces):
    total = None
    for place, piece in zip(places, pieces):
        product = jnp.dot(w_ref[piece_index(place)], piece, preferred_element_type=jnp.float32)
        total = product if total is None else total + product
    return total


def first_kernel(w_ref, *refs):
    piece_refs, (out_ref, mine_ref) = refs[:N_Z], refs[N_Z:]
    width = w_ref.shape[1]
    pieces = [piece_ref[...] for piece_ref in piece_refs]
    for k, piece in enumerate(pieces):
        mine_ref[width * k : width * k + width] = piece
    out_ref[...] = project(w_ref, range(N_Z), pieces)


def shift_kernel(w_ref, attn_ref, first_ref, other_ref, out_ref):
    width = w_ref.shape[1]
    pieces = [other_ref[width * k : width * k + width] for k in range(N_Z)]
    total = first_ref[...] + project(w_ref, range(N_Z, N_TENSOR), pieces)
    row = jnp.sum(total * attn_ref[...].astype(jnp.float32), axis=0, keepdims=True)
    rows = [row[:, LANES * r : LANES * r + LANES] for r in range(6)]
    block = jnp.concatenate(rows + [jnp.zeros((2, LANES), jnp.float32)], axis=0)
    for k in range(N_TENSOR):
        out_ref[k] = block


def grad_kernel(
    recv_ref,
    aux_ref,
    sums_ref,
    attn_ref,
    mine_ref,
    other_ref,
    out_ref,
):
    width = attn_ref.shape[0]
    shift = jnp.sum(recv_ref[...], axis=0)
    gap, signed, base = aux_ref[0], aux_ref[1], aux_ref[2]
    ratio = jnp.exp(gap + shift)
    loss = jnp.sum(
        jnp.minimum(ratio * signed, jnp.clip(ratio, 1.0 - EPS_LOW, 1.0 + EPS_HIGH) * signed)
    )
    coefficient = base * ratio
    row = jnp.concatenate([coefficient[r : r + 1] for r in range(6)], axis=1)
    scaled = (attn_ref[...].astype(jnp.float32) * row).astype(jnp.bfloat16)
    lane = lax.broadcasted_iota(jnp.int32, (8, LANES), 1)
    is_loss = (lane == 35) | (lane == 39) | (lane == 43)
    value = jnp.where(is_loss, loss, sums_ref[...])
    high = value.astype(jnp.bfloat16).astype(jnp.float32)
    middle = (value - high).astype(jnp.bfloat16).astype(jnp.float32)
    low = value - high - middle
    stats = jnp.where(lane < 36, high, jnp.where(lane < 40, middle, low))[:, 32:]
    for place in range(N_TENSOR):
        k = place % N_Z
        piece = (mine_ref, other_ref)[place // N_Z][width * k : width * k + width]
        product = lax.dot_general(
            piece, scaled, (((1,), (1,)), ((), ())), preferred_element_type=jnp.float32
        )
        block = piece_index(place)
        for q in range(4):
            part = product[40 * q : 40 * q + 40]
            rest = part[:, LANES:]
            first = jnp.concatenate([rest[8 * k : 8 * k + 8] for k in range(4)], axis=1)
            second = jnp.concatenate([rest[32:40], stats], axis=1)
            out_ref[4 * block + q] = jnp.concatenate([part[:, :LANES], first, second], axis=0).astype(
                jnp.bfloat16
            )


def finish_kernel(recv_ref, grad_ref, stats_ref):
    total = jnp.sum(recv_ref[...].astype(jnp.float32), axis=0)
    first, second = total[40:48], total[48:56]
    lane = lax.broadcasted_iota(jnp.int32, (1, LANES), 1)
    row = second[0:1]

    def pick(k):
        mine = (lane == 32 + k) | (lane == 36 + k) | (lane == 40 + k)
        return jnp.sum(jnp.where(mine, row, 0.0), axis=1, keepdims=True)

    divisor = jnp.maximum(pick(0), 1.0)
    rest = jnp.concatenate([first[:, 32 * k : 32 * k + 32] for k in range(4)] + [second[:, :32]], axis=0)
    grad_ref[...] = jnp.concatenate([total[:40], rest], axis=1) / divisor
    stats_ref[...] = (
        jnp.where(lane == 0, -pick(3), jnp.where(lane == 1, pick(1), jnp.where(lane == 2, pick(2), 0.0)))
        / divisor
    )


def body(
    attn_output, readout_vectors, w_out, log_gap, magnitude, reward_sign, keep_mask, move_plan
):
    local_rows, width = attn_output.shape
    attn_t, readout_t = attn_output.T, readout_vectors.T
    up, down, swap = [], [], []
    for z in range(N_Z):
        for c in range(2):
            lower, upper = 2 * z + c, 2 * ((z + 1) % N_Z) + c
            up.append((upper, lower) if c else (lower, upper))
            down.append((lower, upper) if c else (upper, lower))
            swap.append((2 * z + 1 - c, 2 * z + c))
    rising, falling, nearby = readout_t, readout_t, [readout_t]
    for _ in range(3):
        rising = lax.ppermute(rising, "tensor", up)
        falling = lax.ppermute(falling, "tensor", down)
        nearby += [rising, falling]
    nearby.append(lax.ppermute(rising, "tensor", up))

    params = pltpu.CompilerParams(vmem_limit_bytes=24 << 20)
    tiled = (local_rows // LANES, LANES)
    w_blocks, aux, sums = pl.pallas_call(
        prepare_kernel,
        in_specs=[vmem_spec()] * 6,
        out_specs=[vmem_spec()] * 3,
        out_shape=[
            jax.ShapeDtypeStruct((N_TENSOR, width, width), w_out.dtype),
            jax.ShapeDtypeStruct((3, 8, LANES), jnp.float32),
            jax.ShapeDtypeStruct((8, LANES), jnp.float32),
        ],
        compiler_params=params,
    )(
        w_out,
        log_gap.astype(jnp.float32).reshape(tiled),
        magnitude.astype(jnp.float32).reshape(tiled),
        reward_sign.reshape(tiled),
        keep_mask.reshape(tiled),
        move_plan,
    )
    first, mine = pl.pallas_call(
        first_kernel,
        in_specs=[vmem_spec()] * (1 + N_Z),
        out_specs=[vmem_spec()] * 2,
        out_shape=[
            jax.ShapeDtypeStruct((width, local_rows), jnp.float32),
            jax.ShapeDtypeStruct((N_Z * width, local_rows), readout_t.dtype),
        ],
        compiler_params=params,
    )(w_blocks, *nearby)
    other = lax.ppermute(mine, "tensor", swap)
    partial_shift = pl.pallas_call(
        shift_kernel,
        in_specs=[vmem_spec()] * 4,
        out_specs=vmem_spec(),
        out_shape=jax.ShapeDtypeStruct((N_TENSOR, 8, LANES), jnp.float32),
        compiler_params=params,
    )(w_blocks, attn_t, first, other)
    shifts = lax.all_to_all(partial_shift, "tensor", 0, 0, tiled=True)
    chunks = pl.pallas_call(
        grad_kernel,
        in_specs=[vmem_spec()] * 6,
        out_specs=vmem_spec(),
        out_shape=jax.ShapeDtypeStruct((N_DP, CHUNK_ROWS, LANES), jnp.bfloat16),
        compiler_params=params,
    )(shifts, aux, sums, attn_t, mine, other)
    received = lax.all_to_all(chunks, "dp", 0, 0, tiled=True)
    grad_t, stats = pl.pallas_call(
        finish_kernel,
        in_specs=[vmem_spec()],
        out_specs=[vmem_spec(), vmem_spec()],
        out_shape=[
            jax.ShapeDtypeStruct((40, width), jnp.float32),
            jax.ShapeDtypeStruct((1, LANES), jnp.float32),
        ],
        compiler_params=pltpu.CompilerParams(vmem_limit_bytes=24 << 20),
    )(received)
    return grad_t.T, stats[0, :3]


def solution(mesh):
    placed = (
        P("dp", "tensor"),
        P("dp", "tensor"),
        P("tensor", None),
        P("dp"),
        P("dp"),
        P("dp"),
        P("dp"),
        P(),
    )
    return jax.shard_map(
        body, mesh=mesh, in_specs=placed, out_specs=(P("tensor", "dp"), P()), check_vma=False
    )
```

```python
import jax
import jax.numpy as jnp
from jax import lax
from jax.experimental import pallas as pl
from jax.experimental.pallas import tpu as pltpu
from jax.sharding import PartitionSpec as P

EPS_LOW = 0.2
EPS_HIGH = 0.28
LOSS_SCALE = 16384.0
N_DP = 64
N_TENSOR = 16
CHUNK_ROWS = 56
LANES = 128
N_Z = 8
STEPS = (0, -1, 1, -2, 2, -3, 3, 4)


def vmem_spec():
    return pl.BlockSpec(memory_space=pltpu.VMEM)


def piece_index(place):
    device = lax.axis_index("tensor")
    side = (device & 1) ^ (place // N_Z)
    return (((device >> 1) + N_Z + STEPS[place % N_Z]) & (N_Z - 1)) * 2 + side


def prepare_kernel(
    w_ref, gap_ref, size_ref, sign_ref, keep_ref, plan_ref, readout_ref, out_ref, aux_ref, sums_ref, own_ref
):
    own_ref[...] = readout_ref[...]
    width = out_ref.shape[2]
    for k in range(N_TENSOR):
        out_ref[k] = w_ref[:, width * k : width * k + width]
    owner = lax.broadcasted_iota(jnp.int32, plan_ref.shape, 0)
    live_total = jnp.sum(jnp.where(owner == lax.axis_index("dp"), plan_ref[...], 0))
    shape = gap_ref.shape
    slot_ids = lax.broadcasted_iota(jnp.int32, shape, 0) * LANES + lax.broadcasted_iota(jnp.int32, shape, 1)
    weight = jnp.where(slot_ids < live_total, keep_ref[...], 0).astype(jnp.float32)
    gap = gap_ref[...]
    advantage = (2 * sign_ref[...] - 1).astype(jnp.float32) * size_ref[...]
    base_ratio = jnp.exp(gap)
    clip_high = jnp.where((advantage > 0) & (base_ratio > 1.0 + EPS_HIGH), 1.0, 0.0)
    clip_low = jnp.where((advantage < 0) & (base_ratio < 1.0 - EPS_LOW), 1.0, 0.0)
    signed = weight * advantage
    zeros = jnp.zeros((2, LANES), jnp.float32)
    base = -LOSS_SCALE * signed * (1.0 - clip_high - clip_low)
    for k, value in enumerate((gap, signed, base)):
        aux_ref[k] = jnp.concatenate([value, zeros], axis=0)
    lane = lax.broadcasted_iota(jnp.int32, (8, LANES), 1)
    which = jnp.where((lane >= 32) & (lane < 44), lane & 3, 3)
    count, high, low = jnp.sum(weight), jnp.sum(weight * clip_high), jnp.sum(weight * clip_low)
    sums_ref[...] = jnp.where(
        which == 0, count, jnp.where(which == 1, high, jnp.where(which == 2, low, 0.0))
    )


def project(w_ref, places, pieces):
    total = None
    for place, piece in zip(places, pieces):
        product = jnp.dot(w_ref[piece_index(place)], piece, preferred_element_type=jnp.float32)
        total = product if total is None else total + product
    return total


def first_kernel(w_ref, *refs):
    piece_refs, (out_ref, mine_ref) = refs[:N_Z], refs[N_Z:]
    width = w_ref.shape[1]
    pieces = [piece_ref[...] for piece_ref in piece_refs]
    for k, piece in enumerate(pieces):
        mine_ref[width * k : width * k + width] = piece
    out_ref[...] = project(w_ref, range(N_Z), pieces)


def shift_kernel(w_ref, attn_ref, first_ref, other_ref, out_ref):
    width = w_ref.shape[1]
    pieces = [other_ref[width * k : width * k + width] for k in range(N_Z)]
    total = first_ref[...] + project(w_ref, range(N_Z, N_TENSOR), pieces)
    row = jnp.sum(total * attn_ref[...].astype(jnp.float32), axis=0, keepdims=True)
    rows = [row[:, LANES * r : LANES * r + LANES] for r in range(6)]
    block = jnp.concatenate(rows + [jnp.zeros((2, LANES), jnp.float32)], axis=0)
    for k in range(N_TENSOR):
        out_ref[k] = block


def grad_kernel(
    recv_ref,
    aux_ref,
    sums_ref,
    attn_ref,
    mine_ref,
    other_ref,
    out_ref,
):
    width = attn_ref.shape[0]
    shift = jnp.sum(recv_ref[...], axis=0)
    gap, signed, base = aux_ref[0], aux_ref[1], aux_ref[2]
    ratio = jnp.exp(gap + shift)
    loss = jnp.sum(
        jnp.minimum(ratio * signed, jnp.clip(ratio, 1.0 - EPS_LOW, 1.0 + EPS_HIGH) * signed)
    )
    coefficient = base * ratio
    row = jnp.concatenate([coefficient[r : r + 1] for r in range(6)], axis=1)
    scaled = (attn_ref[...].astype(jnp.float32) * row).astype(jnp.bfloat16)
    lane = lax.broadcasted_iota(jnp.int32, (8, LANES), 1)
    is_loss = (lane == 35) | (lane == 39) | (lane == 43)
    value = jnp.where(is_loss, loss, sums_ref[...])
    high = value.astype(jnp.bfloat16).astype(jnp.float32)
    middle = (value - high).astype(jnp.bfloat16).astype(jnp.float32)
    low = value - high - middle
    stats = jnp.where(lane < 36, high, jnp.where(lane < 40, middle, low))[:, 32:]
    for place in range(N_TENSOR):
        k = place % N_Z
        piece = (mine_ref, other_ref)[place // N_Z][width * k : width * k + width]
        product = lax.dot_general(
            piece, scaled, (((1,), (1,)), ((), ())), preferred_element_type=jnp.float32
        )
        block = piece_index(place)
        for q in range(4):
            part = product[40 * q : 40 * q + 40]
            rest = part[:, LANES:]
            first = jnp.concatenate([rest[8 * k : 8 * k + 8] for k in range(4)], axis=1)
            second = jnp.concatenate([rest[32:40], stats], axis=1)
            out_ref[4 * block + q] = jnp.concatenate([part[:, :LANES], first, second], axis=0).astype(
                jnp.bfloat16
            )


def finish_kernel(recv_ref, grad_ref, stats_ref):
    total = jnp.sum(recv_ref[...].astype(jnp.float32), axis=0)
    first, second = total[40:48], total[48:56]
    lane = lax.broadcasted_iota(jnp.int32, (1, LANES), 1)
    row = second[0:1]

    def pick(k):
        mine = (lane == 32 + k) | (lane == 36 + k) | (lane == 40 + k)
        return jnp.sum(jnp.where(mine, row, 0.0), axis=1, keepdims=True)

    divisor = jnp.maximum(pick(0), 1.0)
    rest = jnp.concatenate([first[:, 32 * k : 32 * k + 32] for k in range(4)] + [second[:, :32]], axis=0)
    grad_ref[...] = jnp.concatenate([total[:40], rest], axis=1) / divisor
    for k, part in enumerate((-pick(3), pick(1), pick(2))):
        stats_ref[k] = jnp.sum(part / divisor)


def body(
    attn_output, readout_vectors, w_out, log_gap, magnitude, reward_sign, keep_mask, move_plan
):
    local_rows, width = attn_output.shape
    attn_t, readout_t = attn_output.T, readout_vectors.T
    up, down, swap = [], [], []
    for z in range(N_Z):
        for c in range(2):
            up.append((2 * z + c, 2 * ((z + 1) % N_Z) + c))
            down.append((2 * ((z + 1) % N_Z) + c, 2 * z + c))
            swap.append((2 * z + 1 - c, 2 * z + c))
    rising, falling, nearby = readout_t, readout_t, [readout_t]
    for _ in range(3):
        rising = lax.ppermute(rising, "tensor", up)
        falling = lax.ppermute(falling, "tensor", down)
        nearby += [rising, falling]
    nearby.append(lax.ppermute(rising, "tensor", up))

    params = pltpu.CompilerParams(vmem_limit_bytes=24 << 20)
    tiled = (local_rows // LANES, LANES)
    w_blocks, aux, sums, own = pl.pallas_call(
        prepare_kernel,
        in_specs=[vmem_spec()] * 7,
        out_specs=[vmem_spec()] * 4,
        out_shape=[
            jax.ShapeDtypeStruct((N_TENSOR, width, width), w_out.dtype),
            jax.ShapeDtypeStruct((3, 8, LANES), jnp.float32),
            jax.ShapeDtypeStruct((8, LANES), jnp.float32),
            jax.ShapeDtypeStruct(readout_t.shape, readout_t.dtype),
        ],
        compiler_params=params,
    )(
        w_out,
        log_gap.astype(jnp.float32).reshape(tiled),
        magnitude.astype(jnp.float32).reshape(tiled),
        reward_sign.reshape(tiled),
        keep_mask.reshape(tiled),
        move_plan,
        readout_t,
    )
    first, mine = pl.pallas_call(
        first_kernel,
        in_specs=[vmem_spec()] * (1 + N_Z),
        out_specs=[vmem_spec()] * 2,
        out_shape=[
            jax.ShapeDtypeStruct((width, local_rows), jnp.float32),
            jax.ShapeDtypeStruct((N_Z * width, local_rows), readout_t.dtype),
        ],
        compiler_params=params,
    )(w_blocks, own, *nearby[1:])
    other = lax.ppermute(mine, "tensor", swap)
    partial_shift = pl.pallas_call(
        shift_kernel,
        in_specs=[vmem_spec()] * 4,
        out_specs=vmem_spec(),
        out_shape=jax.ShapeDtypeStruct((N_TENSOR, 8, LANES), jnp.float32),
        compiler_params=params,
    )(w_blocks, attn_t, first, other)
    shifts = lax.all_to_all(partial_shift, "tensor", 0, 0, tiled=True)
    chunks = pl.pallas_call(
        grad_kernel,
        in_specs=[vmem_spec()] * 6,
        out_specs=vmem_spec(),
        out_shape=jax.ShapeDtypeStruct((N_DP, CHUNK_ROWS, LANES), jnp.bfloat16),
        compiler_params=params,
    )(shifts, aux, sums, attn_t, mine, other)
    received = lax.all_to_all(chunks, "dp", 0, 0, tiled=True)
    grad_t, stats = pl.pallas_call(
        finish_kernel,
        in_specs=[vmem_spec()],
        out_specs=[vmem_spec(), pl.BlockSpec(memory_space=pltpu.SMEM)],
        out_shape=[
            jax.ShapeDtypeStruct((40, width), jnp.float32),
            jax.ShapeDtypeStruct((3,), jnp.float32),
        ],
        compiler_params=pltpu.CompilerParams(vmem_limit_bytes=24 << 20),
    )(received)
    return grad_t.T, stats


def solution(mesh):
    placed = (
        P("dp", "tensor"),
        P("dp", "tensor"),
        P("tensor", None),
        P("dp"),
        P("dp"),
        P("dp"),
        P("dp"),
        P(),
    )
    return jax.shard_map(
        body, mesh=mesh, in_specs=placed, out_specs=(P("tensor", "dp"), P()), check_vma=False
    )
```

```python
import jax
import jax.numpy as jnp
from jax import lax
from jax.experimental import pallas as pl
from jax.experimental.pallas import tpu as pltpu
from jax.sharding import PartitionSpec as P

EPS_LOW = 0.2
EPS_HIGH = 0.28
LOSS_SCALE = 16384.0
N_DP = 64
N_TENSOR = 16
CHUNK_ROWS = 56
LANES = 128
N_Z = 8
STEPS = (0, -1, 1, -2, 2, -3, 3, 4)


def vmem_spec():
    return pl.BlockSpec(memory_space=pltpu.VMEM)


def piece_index(place):
    device = lax.axis_index("tensor")
    side = (device & 1) ^ (place // N_Z)
    return (((device >> 1) + N_Z + STEPS[place % N_Z]) & (N_Z - 1)) * 2 + side


def prepare_kernel(
    w_ref, rows_ref, plan_ref, readout_ref, out_ref, aux_ref, sums_ref, own_ref
):
    own_ref[...] = readout_ref[...]
    width = out_ref.shape[2]
    for k in range(N_TENSOR):
        out_ref[k] = w_ref[:, width * k : width * k + width]
    owner = lax.broadcasted_iota(jnp.int32, plan_ref.shape, 0)
    live_total = jnp.sum(jnp.where(owner == lax.axis_index("dp"), plan_ref[...], 0))
    gap, size, sign, keep = (rows_ref[k] for k in range(4))
    shape = gap.shape
    slot_ids = lax.broadcasted_iota(jnp.int32, shape, 0) * LANES + lax.broadcasted_iota(jnp.int32, shape, 1)
    weight = jnp.where(slot_ids < live_total, keep, 0.0)
    advantage = (2.0 * sign - 1.0) * size
    base_ratio = jnp.exp(gap)
    clip_high = jnp.where((advantage > 0) & (base_ratio > 1.0 + EPS_HIGH), 1.0, 0.0)
    clip_low = jnp.where((advantage < 0) & (base_ratio < 1.0 - EPS_LOW), 1.0, 0.0)
    signed = weight * advantage
    zeros = jnp.zeros((2, LANES), jnp.float32)
    base = -LOSS_SCALE * signed * (1.0 - clip_high - clip_low)
    for k, value in enumerate((gap, signed, base)):
        aux_ref[k] = jnp.concatenate([value, zeros], axis=0)
    lane = lax.broadcasted_iota(jnp.int32, (8, LANES), 1)
    which = jnp.where((lane >= 32) & (lane < 44), lane & 3, 3)
    count, high, low = jnp.sum(weight), jnp.sum(weight * clip_high), jnp.sum(weight * clip_low)
    sums_ref[...] = jnp.where(
        which == 0, count, jnp.where(which == 1, high, jnp.where(which == 2, low, 0.0))
    )


def project(w_ref, places, pieces):
    total = None
    for place, piece in zip(places, pieces):
        product = jnp.dot(w_ref[piece_index(place)], piece, preferred_element_type=jnp.float32)
        total = product if total is None else total + product
    return total


def first_kernel(w_ref, *refs):
    piece_refs, (out_ref, mine_ref) = refs[:N_Z], refs[N_Z:]
    width = w_ref.shape[1]
    pieces = [piece_ref[...] for piece_ref in piece_refs]
    for k, piece in enumerate(pieces):
        mine_ref[width * k : width * k + width] = piece
    out_ref[...] = project(w_ref, range(N_Z), pieces)


def shift_kernel(w_ref, attn_ref, first_ref, other_ref, out_ref):
    width = w_ref.shape[1]
    pieces = [other_ref[width * k : width * k + width] for k in range(N_Z)]
    total = first_ref[...] + project(w_ref, range(N_Z, N_TENSOR), pieces)
    row = jnp.sum(total * attn_ref[...].astype(jnp.float32), axis=0, keepdims=True)
    rows = [row[:, LANES * r : LANES * r + LANES] for r in range(6)]
    block = jnp.concatenate(rows + [jnp.zeros((2, LANES), jnp.float32)], axis=0)
    for k in range(N_TENSOR):
        out_ref[k] = block


def grad_kernel(
    recv_ref,
    aux_ref,
    sums_ref,
    attn_ref,
    mine_ref,
    other_ref,
    out_ref,
):
    width = attn_ref.shape[0]
    shift = jnp.sum(recv_ref[...], axis=0)
    gap, signed, base = aux_ref[0], aux_ref[1], aux_ref[2]
    ratio = jnp.exp(gap + shift)
    loss = jnp.sum(
        jnp.minimum(ratio * signed, jnp.clip(ratio, 1.0 - EPS_LOW, 1.0 + EPS_HIGH) * signed)
    )
    coefficient = base * ratio
    row = jnp.concatenate([coefficient[r : r + 1] for r in range(6)], axis=1)
    scaled = (attn_ref[...].astype(jnp.float32) * row).astype(jnp.bfloat16)
    lane = lax.broadcasted_iota(jnp.int32, (8, LANES), 1)
    is_loss = (lane == 35) | (lane == 39) | (lane == 43)
    value = jnp.where(is_loss, loss, sums_ref[...])
    high = value.astype(jnp.bfloat16).astype(jnp.float32)
    middle = (value - high).astype(jnp.bfloat16).astype(jnp.float32)
    low = value - high - middle
    stats = jnp.where(lane < 36, high, jnp.where(lane < 40, middle, low))[:, 32:]
    for place in range(N_TENSOR):
        k = place % N_Z
        piece = (mine_ref, other_ref)[place // N_Z][width * k : width * k + width]
        product = lax.dot_general(
            piece, scaled, (((1,), (1,)), ((), ())), preferred_element_type=jnp.float32
        )
        block = piece_index(place)
        for q in range(4):
            part = product[40 * q : 40 * q + 40]
            rest = part[:, LANES:]
            first = jnp.concatenate([rest[8 * k : 8 * k + 8] for k in range(4)], axis=1)
            second = jnp.concatenate([rest[32:40], stats], axis=1)
            out_ref[4 * block + q] = jnp.concatenate([part[:, :LANES], first, second], axis=0).astype(
                jnp.bfloat16
            )


def finish_kernel(recv_ref, grad_ref, stats_ref):
    total = jnp.sum(recv_ref[...].astype(jnp.float32), axis=0)
    first, second = total[40:48], total[48:56]
    lane = lax.broadcasted_iota(jnp.int32, (1, LANES), 1)
    row = second[0:1]

    def pick(k):
        mine = (lane == 32 + k) | (lane == 36 + k) | (lane == 40 + k)
        return jnp.sum(jnp.where(mine, row, 0.0), axis=1, keepdims=True)

    divisor = jnp.maximum(pick(0), 1.0)
    rest = jnp.concatenate([first[:, 32 * k : 32 * k + 32] for k in range(4)] + [second[:, :32]], axis=0)
    grad_ref[...] = jnp.concatenate([total[:40], rest], axis=1) / divisor
    for k, part in enumerate((-pick(3), pick(1), pick(2))):
        stats_ref[k] = jnp.sum(part / divisor)


def body(
    attn_output, readout_vectors, w_out, log_gap, magnitude, reward_sign, keep_mask, move_plan
):
    local_rows, width = attn_output.shape
    attn_t, readout_t = attn_output.T, readout_vectors.T
    up, down, swap = [], [], []
    for z in range(N_Z):
        for c in range(2):
            up.append((2 * z + c, 2 * ((z + 1) % N_Z) + c))
            down.append((2 * ((z + 1) % N_Z) + c, 2 * z + c))
            swap.append((2 * z + 1 - c, 2 * z + c))
    rising, falling, nearby = readout_t, readout_t, [readout_t]
    for _ in range(3):
        rising = lax.ppermute(rising, "tensor", up)
        falling = lax.ppermute(falling, "tensor", down)
        nearby += [rising, falling]
    nearby.append(lax.ppermute(rising, "tensor", up))

    params = pltpu.CompilerParams(vmem_limit_bytes=24 << 20)
    tiled = (local_rows // LANES, LANES)
    w_blocks, aux, sums, own = pl.pallas_call(
        prepare_kernel,
        in_specs=[vmem_spec()] * 4,
        out_specs=[vmem_spec()] * 4,
        out_shape=[
            jax.ShapeDtypeStruct((N_TENSOR, width, width), w_out.dtype),
            jax.ShapeDtypeStruct((3, 8, LANES), jnp.float32),
            jax.ShapeDtypeStruct((8, LANES), jnp.float32),
            jax.ShapeDtypeStruct(readout_t.shape, readout_t.dtype),
        ],
        compiler_params=params,
    )(
        w_out,
        jnp.stack(
            [
                row.astype(jnp.float32).reshape(tiled)
                for row in (log_gap, magnitude, reward_sign, keep_mask)
            ]
        ),
        move_plan,
        readout_t,
    )
    first, mine = pl.pallas_call(
        first_kernel,
        in_specs=[vmem_spec()] * (1 + N_Z),
        out_specs=[vmem_spec()] * 2,
        out_shape=[
            jax.ShapeDtypeStruct((width, local_rows), jnp.float32),
            jax.ShapeDtypeStruct((N_Z * width, local_rows), readout_t.dtype),
        ],
        compiler_params=params,
    )(w_blocks, own, *nearby[1:])
    other = lax.ppermute(mine, "tensor", swap)
    partial_shift = pl.pallas_call(
        shift_kernel,
        in_specs=[vmem_spec()] * 4,
        out_specs=vmem_spec(),
        out_shape=jax.ShapeDtypeStruct((N_TENSOR, 8, LANES), jnp.float32),
        compiler_params=params,
    )(w_blocks, attn_t, first, other)
    shifts = lax.all_to_all(partial_shift, "tensor", 0, 0, tiled=True)
    chunks = pl.pallas_call(
        grad_kernel,
        in_specs=[vmem_spec()] * 6,
        out_specs=vmem_spec(),
        out_shape=jax.ShapeDtypeStruct((N_DP, CHUNK_ROWS, LANES), jnp.bfloat16),
        compiler_params=params,
    )(shifts, aux, sums, attn_t, mine, other)
    received = lax.all_to_all(chunks, "dp", 0, 0, tiled=True)
    grad_t, stats = pl.pallas_call(
        finish_kernel,
        in_specs=[vmem_spec()],
        out_specs=[vmem_spec(), pl.BlockSpec(memory_space=pltpu.SMEM)],
        out_shape=[
            jax.ShapeDtypeStruct((40, width), jnp.float32),
            jax.ShapeDtypeStruct((3,), jnp.float32),
        ],
        compiler_params=pltpu.CompilerParams(vmem_limit_bytes=24 << 20),
    )(received)
    return grad_t.T, stats


def solution(mesh):
    placed = (
        P("dp", "tensor"),
        P("dp", "tensor"),
        P("tensor", None),
        P("dp"),
        P("dp"),
        P("dp"),
        P("dp"),
        P(),
    )
    return jax.shard_map(
        body, mesh=mesh, in_specs=placed, out_specs=(P("tensor", "dp"), P()), check_vma=False
    )
```
